256 devices in a mesh: gx: 32 (over x_lo, z, core), gy: 8 (over x_hi, y).
Axes of the slice: x: 4 (x_hi: 2, x_lo: 2; x = x_hi * 2 + x_lo), y: 4, z: 8, core: 2. Of those that a mesh axis runs over, the one named last changes fastest.
Arguments:
- angles: float32 [8, 4, 512, 2048], P(None, None, 'gx', 'gy'), may hold values from -3.140625 to 3.140625
- bond_flux: int32 [7, 512, 2048], P(None, 'gx', 'gy'), may hold values from 0 to 63
- coupling: float32 [512, 2048], P('gx', 'gy'), may hold values from 0.2 to 0.8
Outputs:
- evolved: float32 [2, 8, 4, 512, 2048], P(None, None, None, 'gx', 'gy')
- moments: float32 [16, 2, 8], replicated
The draws below stay inside these ranges and needn't reach their ends.
All inputs are finite; a program needn't handle non-finite values.
Results may differ from the reference program's by a relative error of at most 0.0003.
Values sent between devices are 32-bit elements; how exact they have to be, the bound alone decides.
A program may use at most 192 MiB of HBM per device.

```python
import math
import jax
import jax.numpy as jnp
from jax import lax

STATES = 8
TERMS = 16
QUANTA = 64
NX = 512
NY = 2048


def with_ends(entries, own_key, low, high):
    longest = entries.shape.index(max(entries.shape))
    spots = []
    for shift in (0, 1):
        where = [jax.random.randint(jax.random.fold_in(own_key, axis), (), 0, length) for axis, length in enumerate(entries.shape)]
        where[longest] = (where[longest] + shift) % entries.shape[longest]
        spots.append(tuple(where))
    return entries.at[spots[0]].set(low).at[spots[1]].set(high)


def levels(own_key, dims, cuts, least, largest):
    def one(axis_at, blocks):
        heights = jax.random.uniform(jax.random.fold_in(jax.random.fold_in(own_key, 6), axis_at), (blocks,), jnp.float32, least / len(cuts), largest / len(cuts))
        return jnp.repeat(jnp.exp(heights), dims[axis_at] // blocks).reshape((-1,) + (1,) * (len(dims) - axis_at - 1))

    loudness = one(*cuts[0])
    for cut in cuts[1:]:
        loudness = loudness * one(*cut)
    return loudness


def setup_inputs(seed: int = 0) -> dict:
    key_of = jax.random.split(jax.random.key(seed), 4)
    return {
        "angles": jnp.clip(jax.random.uniform(key_of[0], (STATES, 4, NX, NY), jnp.float32, -3.140625, 3.140625), -3.140625, 3.140625),
        "bond_flux": with_ends(jax.random.randint(key_of[1], (7, NX, NY), 0, QUANTA), jax.random.fold_in(key_of[1], 1), 0, QUANTA - 1).astype(jnp.int32),
        "coupling": jnp.clip(0.2 + 0.6 * jax.random.uniform(key_of[2], (NX, NY), jnp.float32) ** levels(key_of[2], (NX, NY), ((0, 32), (1, 8)), -0.2, 0.2), 0.2, 0.8),
    }


energy_scale = 4.0
phase_span = 12.0

def bessel_value(degree, argument):
    running = 0.0
    for number in range(60):
        running += (-1.0) ** number * (argument / 2.0) ** (2 * number + degree) / (math.factorial(number) * math.factorial(number + degree))
    return running

def chebyshev_weights(count):
    weights_real = []
    weights_imag = []
    for degree in range(count):
        amplitude = bessel_value(degree, phase_span) * (1.0 if degree == 0 else 2.0)
        quarter = degree % 4
        weights_real.append(amplitude if quarter == 0 else -amplitude if quarter == 2 else 0.0)
        weights_imag.append(-amplitude if quarter == 1 else amplitude if quarter == 3 else 0.0)
    return (weights_real, weights_imag)

def rotate(cosine_part, sine_part, pair, sign):
    return (cosine_part * pair[0] - sign * sine_part * pair[1], sign * sine_part * pair[0] + cosine_part * pair[1])

def orbital(complex_field, position):
    return (complex_field[0][:, position], complex_field[1][:, position])

def summed(one_pair, two_pair, three_pair):
    return (one_pair[0] + two_pair[0] + three_pair[0], one_pair[1] + two_pair[1] + three_pair[1])

def negated(pair):
    return (-pair[0], -pair[1])

def times_unit(pair):
    return (-pair[1], pair[0])

def assemble(site_a1, site_b2, site_b1, site_a2):
    real_part = jnp.stack([site_a1[0], site_b2[0], site_b1[0], site_a2[0]], axis=1)
    imag_part = jnp.stack([site_a1[1], site_b2[1], site_b1[1], site_a2[1]], axis=1)
    return jnp.stack([real_part, imag_part])

def apply_ham(state_field, nearby, tables):
    lower_x, upper_x, lower_y, upper_y = nearby
    cos_own, sin_own, cos_near, sin_near, coupling = tables
    site_a1 = negated(summed(rotate(cos_own[0], sin_own[0], orbital(state_field, 2), 1.0), rotate(cos_own[1], sin_own[1], orbital(lower_x, 0), 1.0), rotate(cos_own[2], sin_own[2], orbital(lower_y, 0), 1.0)))
    site_b2 = negated(summed(rotate(cos_own[3], sin_own[3], orbital(state_field, 3), -1.0), rotate(cos_near[2], sin_near[2], orbital(lower_x, 1), -1.0), rotate(cos_near[3], sin_near[3], orbital(lower_y, 1), -1.0)))
    hop_b1 = negated(summed(rotate(cos_own[0], sin_own[0], orbital(state_field, 0), -1.0), rotate(cos_near[0], sin_near[0], orbital(upper_x, 0), -1.0), rotate(cos_near[1], sin_near[1], orbital(upper_y, 0), -1.0)))
    inter_b1 = rotate(cos_own[6], sin_own[6], orbital(state_field, 3), 1.0)
    site_b1 = (hop_b1[0] + coupling * inter_b1[0], hop_b1[1] + coupling * inter_b1[1])
    hop_a2 = negated(summed(rotate(cos_own[3], sin_own[3], orbital(state_field, 1), 1.0), rotate(cos_own[4], sin_own[4], orbital(upper_x, 1), 1.0), rotate(cos_own[5], sin_own[5], orbital(upper_y, 1), 1.0)))
    inter_a2 = rotate(cos_own[6], sin_own[6], orbital(state_field, 2), -1.0)
    site_a2 = (hop_a2[0] + coupling * inter_a2[0], hop_a2[1] + coupling * inter_a2[1])
    return assemble(site_a1, site_b2, site_b1, site_a2)

def apply_vel(state_field, nearby, tables):
    lower_x, upper_x, lower_y, upper_y = nearby
    cos_own, sin_own, cos_near, sin_near, coupling = tables
    site_a1 = times_unit(negated(rotate(cos_own[1], sin_own[1], orbital(lower_x, 0), 1.0)))
    site_b1 = times_unit(rotate(cos_near[0], sin_near[0], orbital(upper_x, 0), -1.0))
    site_a2 = times_unit(rotate(cos_own[4], sin_own[4], orbital(upper_x, 1), 1.0))
    site_b2 = times_unit(negated(rotate(cos_near[2], sin_near[2], orbital(lower_x, 1), -1.0)))
    return assemble(site_a1, site_b2, site_b1, site_a2)

def intersection(velocity, current):
    real_part = lax.optimization_barrier(jnp.sum(velocity[0] * current[0] + velocity[1] * current[1], axis=(1, 2, 3)))
    imag_part = lax.optimization_barrier(jnp.sum(velocity[0] * current[1] - velocity[1] * current[0], axis=(1, 2, 3)))
    return jnp.stack([real_part, imag_part])

def scaled(complex_field, weight_real, weight_imag):
    return jnp.stack([weight_real * complex_field[0] - weight_imag * complex_field[1], weight_real * complex_field[1] + weight_imag * complex_field[0]])

def neighbours(state_field):
    lower_x = jnp.pad(state_field[:, :, 2:4], ((0, 0), (0, 0), (0, 0), (1, 0), (0, 0)))[:, :, :, :-1, :]
    upper_x = jnp.pad(state_field[:, :, 0:2], ((0, 0), (0, 0), (0, 0), (0, 1), (0, 0)))[:, :, :, 1:, :]
    lower_y = jnp.pad(state_field[:, :, 2:4], ((0, 0), (0, 0), (0, 0), (0, 0), (1, 0)))[:, :, :, :, :-1]
    upper_y = jnp.pad(state_field[:, :, 0:2], ((0, 0), (0, 0), (0, 0), (0, 0), (0, 1)))[:, :, :, :, 1:]
    return (lower_x, upper_x, lower_y, upper_y)

def reference(angles, bond_flux, coupling):
    phase_step = 2.0 * math.pi / QUANTA
    theta = bond_flux.astype(jnp.float32) * phase_step
    near_flux = jnp.stack([jnp.pad(bond_flux[1], ((0, 1), (0, 0)))[1:, :], jnp.pad(bond_flux[2], ((0, 0), (0, 1)))[:, 1:], jnp.pad(bond_flux[4], ((1, 0), (0, 0)))[:-1, :], jnp.pad(bond_flux[5], ((0, 0), (1, 0)))[:, :-1]])
    theta_near = near_flux.astype(jnp.float32) * phase_step
    tables = (jnp.cos(theta), jnp.sin(theta), jnp.cos(theta_near), jnp.sin(theta_near), coupling)
    weights_real, weights_imag = chebyshev_weights(TERMS)
    norm_factor = 1.0 / math.sqrt(4.0 * NX * NY)

    def evolve_one(angle_block):
        start = jnp.stack([jnp.cos(angle_block), jnp.sin(angle_block)])[:, None]
        velocity = apply_vel(start, neighbours(start), tables)
        gathered = [intersection(velocity, start)]
        total_sum = scaled(start, weights_real[0], weights_imag[0])
        previous = start
        current = apply_ham(start, neighbours(start), tables) / energy_scale
        total_sum = total_sum + scaled(current, weights_real[1], weights_imag[1])
        gathered.append(intersection(velocity, current))
        for degree in range(2, TERMS):
            following = 2.0 * apply_ham(current, neighbours(current), tables) / energy_scale - previous
            total_sum = total_sum + scaled(following, weights_real[degree], weights_imag[degree])
            gathered.append(intersection(velocity, following))
            previous, current = (current, following)
        return (total_sum[:, 0], jnp.stack(gathered)[:, :, 0] * norm_factor)
    outputs, moment_rows = lax.map(evolve_one, angles)
    evolved = jnp.transpose(outputs, (1, 0, 2, 3, 4))
    moments = jnp.transpose(moment_rows, (1, 2, 0))
    return (evolved, moments)
```

```python
import functools
import math

import jax
import jax.numpy as jnp
from jax import lax
from jax.experimental import pallas as pl
from jax.experimental.pallas import tpu as pltpu
from jax.sharding import PartitionSpec as P

TERMS = 16
QUANTA = 64
PHASE_SPAN = 12.0

STATES = 8
ROWS = 16
COLS = 256
LANES = 128
HALO = 8
EXT = ROWS + 2 * HALO
PAD = EXT + 8
TILES = 3
A1, B2, B1, A2 = 0, 1, 2, 3
MESH = pl.DeviceIdType.MESH

T1C, T1S, T2C, T2S, T2BC, T2BS, T4C, T4S, T5C, T5S, T5BC, T5BS, CPL = range(13)


def bessel_value(degree, argument):
    running = 0.0
    for number in range(60):
        running += (
            (-1.0) ** number
            * (argument / 2.0) ** (2 * number + degree)
            / (math.factorial(number) * math.factorial(number + degree))
        )
    return running


EVEN = [(1.0 if m == 0 else 2.0) * (-1.0) ** m * bessel_value(2 * m, PHASE_SPAN) for m in range(TERMS // 2)]
ODD = [-2.0 * (-1.0) ** m * bessel_value(2 * m + 1, PHASE_SPAN) for m in range(TERMS // 2)]

SIN_COEF = [(-1.0) ** n * math.pi ** (2 * n + 1) / math.factorial(2 * n + 1) for n in range(6)]
COS_COEF = [(-1.0) ** n * math.pi ** (2 * n) / math.factorial(2 * n) for n in range(7)]


def turn(f):
    r = f - jnp.floor(f + 0.5)
    q = r * r
    s = SIN_COEF[-1]
    for value in reversed(SIN_COEF[:-1]):
        s = s * q + value
    s = s * r
    c = COS_COEF[-1]
    for value in reversed(COS_COEF[:-1]):
        c = c * q + value
    return 1.0 - 2.0 * s * s, 2.0 * s * c


def pick(table, m):
    value = jnp.float32(table[0])
    for at in range(1, len(table)):
        value = jnp.where(m == at, jnp.float32(table[at]), value)
    return value


def rot(c, s, v):
    return c * v[0] - s * v[1], s * v[0] + c * v[1]


def rot_back(c, s, v):
    return c * v[0] + s * v[1], c * v[1] - s * v[0]


def add(*pairs):
    re, im = pairs[0]
    for pair in pairs[1:]:
        re, im = re + pair[0], im + pair[1]
    return re, im


def kernel(
    nx, ny, gx_size, gy_size,
    ang_h, flux_h, coup_h, evo_h, mom_ref,
    ang, fli, flf, u, tab, phi, gauge, mask, vel, tot, outv, mom, pack, got, msg_x, msg_y, in_x, in_y,
    load_sem, out_sem, xs_sem, xr_sem, ps_sem, pr_sem, rxs_sem, rxr_sem, rys_sem, ryr_sem,
):
    gx, gy = lax.axis_index("gx"), lax.axis_index("gy")

    def near(dx, dy):
        return (lax.rem(gx + dx + gx_size, gx_size), lax.rem(gy + dy + gy_size, gy_size))

    lane = lax.broadcasted_iota(jnp.int32, (STATES, LANES), 1)
    first_lane, last_lane = lane == 0, lane == LANES - 1

    loads = []
    for t in range(2):
        span = pl.ds(t * LANES, LANES)
        own = pl.ds(HALO, ROWS)
        loads.append(pltpu.make_async_copy(flux_h.at[:, :, span], fli.at[t, :, own, :], load_sem.at[t, 0]))
        loads.append(pltpu.make_async_copy(coup_h.at[:, span], flf.at[t, pl.ds(7 * PAD + HALO, ROWS), :], load_sem.at[t, 1]))
        loads.append(pltpu.make_async_copy(ang_h.at[:, :, :, span], ang.at[t, :, :, own, :], load_sem.at[t, 2]))
    for copy in loads:
        copy.start()

    barrier = pltpu.get_barrier_semaphore()

    def greet_x(d, carry):
        pl.semaphore_signal(barrier, inc=1, device_id=(lax.rem(gx + d, gx_size), gy), device_id_type=MESH)
        return carry

    def greet_y(d, carry):
        pl.semaphore_signal(barrier, inc=1, device_id=(gx, lax.rem(gy + d, gy_size)), device_id_type=MESH)
        return carry

    lax.fori_loop(1, gx_size, greet_x, 0)
    lax.fori_loop(1, gy_size, greet_y, 0)
    for dx in (-1, 1):
        for dy in (-1, 1):
            pl.semaphore_signal(barrier, inc=1, device_id=near(dx, dy), device_id_type=MESH)

    zero = jnp.zeros((STATES, LANES), jnp.float32)
    for t in range(TILES):
        for plane in range(8):
            flf[t, pl.ds(plane * PAD + EXT, 8), :] = zero
        for comp in range(8):
            u[1, comp, t, 0] = zero
            u[1, comp, t, EXT - 1] = zero

    pl.semaphore_wait(barrier, gx_size - 1 + gy_size - 1 + 4)

    row_copies = []
    for side, dx in ((0, 1), (1, -1)):
        src_rows = pl.ds(ROWS - HALO, HALO) if side == 0 else pl.ds(0, HALO)
        low = 0 if side == 0 else HALO + ROWS
        for t in range(2):
            span = pl.ds(t * LANES, LANES)
            for what, (src, dst) in enumerate(
                (
                    (flux_h.at[:, src_rows, span], fli.at[t, :, pl.ds(low, HALO), :]),
                    (coup_h.at[src_rows, span], flf.at[t, pl.ds(7 * PAD + low, HALO), :]),
                    (ang_h.at[:, :, src_rows, span], ang.at[t, :, :, pl.ds(low, HALO), :]),
                )
            ):
                row_copies.append(
                    (
                        what,
                        pltpu.make_async_remote_copy(
                            src_ref=src,
                            dst_ref=dst,
                            send_sem=xs_sem.at[side, t, what],
                            recv_sem=xr_sem.at[side, t, what],
                            device_id=near(dx, 0),
                            device_id_type=MESH,
                        ),
                    )
                )
    for wanted in range(3):
        for what, copy in row_copies:
            if what == wanted:
                copy.start()

    for copy in loads:
        copy.wait()

    def flux_to_float(t, start, count):
        for plane in range(7):
            flf[t, pl.ds(plane * PAD + start, count), :] = fli[t, plane, pl.ds(start, count), :].astype(jnp.float32)

    for t in range(2):
        flux_to_float(t, HALO, ROWS)

    ang_rows = [ang.at[t].reshape(STATES * 4 * EXT, LANES) for t in range(2)]

    def ang_row(t, orb, row):
        return ang_rows[t][pl.ds(orb * EXT + row, STATES, stride=4 * EXT), :]

    group = lane // HALO
    for side in range(2):
        t = 1 - side
        for what in range(5):
            packed = zero
            for row in range(ROWS):
                if what < 4:
                    value = ang_row(t, what, HALO + row)
                else:
                    value = flf[t, pl.ds(HALO + row, 8, stride=PAD), :]
                move = (row * HALO - (LANES - HALO if side == 0 else 0)) % LANES
                if move:
                    value = pltpu.roll(value, move, 1)
                packed = jnp.where(group == row, value, packed)
            pack[side, what] = packed
    pack_copies = []
    for side, dy in ((0, 1), (1, -1)):
        for dx in (0, -1, 1):
            pack_copies.append(
                pltpu.make_async_remote_copy(
                    src_ref=pack.at[side],
                    dst_ref=got.at[side, 1 - dx],
                    send_sem=ps_sem.at[side, 1 - dx],
                    recv_sem=pr_sem.at[side, 1 - dx],
                    device_id=near(dx, dy),
                    device_id_type=MESH,
                )
            )
    for copy in pack_copies:
        copy.start()

    def flux_of(t, plane, start, count=8):
        return flf[t, pl.ds(plane * PAD + start, count), :]

    def gauge_phases(t, start):
        th0, th3, th6 = (flux_of(t, plane, start) for plane in (0, 3, 6))
        phi[0, t, pl.ds(start, 8), :] = 0.5 - th0 * (1.0 / QUANTA)
        phi[1, t, pl.ds(start, 8), :] = 0.5 + (th6 + th3) * (1.0 / QUANTA)
        phi[2, t, pl.ds(start, 8), :] = th6 * (1.0 / QUANTA)

    phi_of = {A1: 0, B2: 1, A2: 2}

    def start_value(angle, orb, t, row):
        f = angle * (0.5 / math.pi)
        if orb != B1:
            f = f + phi[phi_of[orb], t, pl.ds(row, 1), :]
        return turn(f)

    for t in range(2):
        for start in (HALO, HALO + 8):
            gauge_phases(t, start)
            for which in range(3):
                c, s = turn(phi[which, t, pl.ds(start, 8), :])
                gauge[which, 0, t, pl.ds(start - HALO, 8), :] = c
                gauge[which, 1, t, pl.ds(start - HALO, 8), :] = s

    def own_start(row, carry):
        for t in range(2):
            for orb in range(4):
                c, s = start_value(ang_row(t, orb, row), orb, t, row)
                u[0, 2 * orb, t, row] = c
                u[0, 2 * orb + 1, t, row] = s
        return carry

    lax.fori_loop(HALO, HALO + ROWS, own_start, 0)

    for what, copy in row_copies:
        if what < 2:
            copy.wait()
    for t in range(2):
        for start in (0, HALO + ROWS):
            flux_to_float(t, start, HALO)
            gauge_phases(t, start)
    for copy in pack_copies:
        copy.wait()

    def unpack(what, row):
        if row < HALO:
            part, place = 0, row + ROWS - HALO
        elif row < HALO + ROWS:
            part, place = 1, row - HALO
        else:
            part, place = 2, row - HALO - ROWS
        before, after = got[0, part, what], got[1, part, what]
        shift = (LANES - HALO - place * HALO) % LANES
        before = pltpu.roll(before, shift, 1) if shift else before
        shift = (-place * HALO) % LANES
        after = pltpu.roll(after, shift, 1) if shift else after
        return jnp.where(lane < HALO, after, jnp.where(lane >= LANES - HALO, before, 0.0))

    for row in range(EXT):
        flf[2, pl.ds(row, 8, stride=PAD), :] = unpack(4, row)
    for start in range(0, EXT, 8):
        gauge_phases(2, start)

    sub = lax.broadcasted_iota(jnp.int32, (8, LANES), 0)

    def inside(t, start, di, dj):
        i = gx * ROWS - HALO + start + sub + di
        if t < 2:
            j = gy * COLS + t * LANES + lane + dj
            good = (j >= 0) & (j < ny)
        else:
            place = lane + dj
            j = gy * COLS + jnp.where(place < LANES // 2, COLS + place, place - LANES)
            good = (j >= 0) & (j < ny) & ((place < HALO) | (place >= LANES - HALO))
        return good & (i >= 0) & (i < nx)

    def right(values):
        rolled = [pltpu.roll(value, 1, 1) for value in values]
        return [jnp.where(first_lane, rolled[(t + TILES - 1) % TILES], rolled[t]) for t in range(TILES)]

    def left(values):
        rolled = [pltpu.roll(value, LANES - 1, 1) for value in values]
        return [jnp.where(last_lane, rolled[(t + 1) % TILES], rolled[t]) for t in range(TILES)]

    for start in range(0, EXT, 8):
        rows = pl.ds(start, 8)
        th = [[flux_of(t, plane, start) for plane in range(8)] for t in range(TILES)]
        far = left([th[t][6] + th[t][3] for t in range(TILES)])
        t2, t5 = [], []
        for t in range(TILES):
            here = inside(t, start, 0, 0)
            mask[t, rows, :] = here.astype(jnp.float32)

            def bond(phase, good):
                c, s = turn(phase * (1.0 / QUANTA))
                return jnp.where(good, 0.5 * c, 0.0), jnp.where(good, 0.5 * s, 0.0)

            c, s = bond(th[t][1] - th[t][0], here & inside(t, start, -1, 0))
            tab[T1C, t, rows, :], tab[T1S, t, rows, :] = c, s
            below = flux_of(t, 6, start + 1) + flux_of(t, 3, start + 1)
            c, s = bond(th[t][4] + th[t][6] - below, here & inside(t, start, 1, 0))
            tab[T4C, t, rows, :], tab[T4S, t, rows, :] = c, s
            t2.append(bond(th[t][2] - th[t][0], here & inside(t, start, 0, -1)))
            t5.append(bond(th[t][5] + th[t][6] - far[t], here & inside(t, start, 0, 1)))
            tab[CPL, t, rows, :] = jnp.where(here, 0.5 * th[t][7], 0.0)
        for part in range(2):
            t2_back = left([t2[t][part] for t in range(TILES)])
            t5_back = right([t5[t][part] for t in range(TILES)])
            for t in range(TILES):
                tab[T2C + part, t, rows, :] = t2[t][part]
                tab[T2BC + part, t, rows, :] = t2_back[t]
                tab[T5C + part, t, rows, :] = t5[t][part]
                tab[T5BC + part, t, rows, :] = t5_back[t]

    for row in range(EXT):
        for orb in range(4):
            c, s = start_value(unpack(orb, row), orb, 2, row)
            m = mask[2, pl.ds(row, 1), :]
            u[0, 2 * orb, 2, row] = c * m
            u[0, 2 * orb + 1, 2, row] = s * m
    for what, copy in row_copies:
        if what == 2:
            copy.wait()

    def rim_start(place, carry):
        for base in (0, HALO + ROWS):
            row = base + place
            for t in range(2):
                m = mask[t, pl.ds(row, 1), :]
                for orb in range(4):
                    c, s = start_value(ang_row(t, orb, row), orb, t, row)
                    u[0, 2 * orb, t, row] = c * m
                    u[0, 2 * orb + 1, t, row] = s * m
        return carry

    lax.fori_loop(0, HALO, rim_start, 0)

    def site(buf, orb, t, row):
        return u[buf, 2 * orb, t, row], u[buf, 2 * orb + 1, t, row]

    def plane(which, t, row):
        return tab[which, t, pl.ds(row, 1), :]

    def velocity(row, carry):
        for t in range(2):
            v = rot(plane(T1C, t, row), plane(T1S, t, row), site(0, B1, t, row - 1))
            vel[2 * A1, t, row - HALO], vel[2 * A1 + 1, t, row - HALO] = v
            v = rot_back(plane(T1C, t, row + 1), plane(T1S, t, row + 1), site(0, A1, t, row + 1))
            vel[2 * B1, t, row - HALO], vel[2 * B1 + 1, t, row - HALO] = -v[0], -v[1]
            v = rot(plane(T4C, t, row), plane(T4S, t, row), site(0, B2, t, row + 1))
            vel[2 * A2, t, row - HALO], vel[2 * A2 + 1, t, row - HALO] = -v[0], -v[1]
            v = rot_back(plane(T4C, t, row - 1), plane(T4S, t, row - 1), site(0, A2, t, row - 1))
            vel[2 * B2, t, row - HALO], vel[2 * B2 + 1, t, row - HALO] = v
        return carry

    lax.fori_loop(HALO, HALO + ROWS, velocity, 0)

    def step_row(src, dst, row, first):
        here = [[site(src, orb, t, row) for orb in range(4)] for t in range(TILES)]

        def shifted(move, orb):
            re = move([here[t][orb][0] for t in range(TILES)])
            im = move([here[t][orb][1] for t in range(TILES)])
            return list(zip(re, im))

        b1_left, a2_left = shifted(right, B1), shifted(right, A2)
        a1_right, b2_right = shifted(left, A1), shifted(left, B2)
        for t in range(TILES):
            a1, b2, b1, a2 = here[t]
            cpl = plane(CPL, t, row)
            new = [None] * 4
            new[A1] = add(
                (0.5 * b1[0], 0.5 * b1[1]),
                rot(plane(T1C, t, row), plane(T1S, t, row), site(src, B1, t, row - 1)),
                rot(plane(T2C, t, row), plane(T2S, t, row), b1_left[t]),
            )
            new[B1] = add(
                (0.5 * a1[0], 0.5 * a1[1]),
                rot_back(plane(T1C, t, row + 1), plane(T1S, t, row + 1), site(src, A1, t, row + 1)),
                rot_back(plane(T2BC, t, row), plane(T2BS, t, row), a1_right[t]),
                (cpl * a2[0], cpl * a2[1]),
            )
            new[A2] = add(
                (0.5 * b2[0], 0.5 * b2[1]),
                rot(plane(T4C, t, row), plane(T4S, t, row), site(src, B2, t, row + 1)),
                rot(plane(T5C, t, row), plane(T5S, t, row), b2_right[t]),
                (cpl * b1[0], cpl * b1[1]),
            )
            new[B2] = add(
                (0.5 * a2[0], 0.5 * a2[1]),
                rot_back(plane(T4C, t, row - 1), plane(T4S, t, row - 1), site(src, A2, t, row - 1)),
                rot_back(plane(T5BC, t, row), plane(T5BS, t, row), a2_left[t]),
            )
            for orb in range(4):
                for part in range(2):
                    if first:
                        u[dst, 2 * orb + part, t, row] = 0.5 * new[orb][part]
                    else:
                        u[dst, 2 * orb + part, t, row] = new[orb][part] - u[dst, 2 * orb + part, t, row]

    def step(src, dst, low, pairs, first=False):
        def two_rows(at, carry):
            step_row(src, dst, low + 2 * at, first)
            step_row(src, dst, low + 2 * at + 1, first)
            return carry

        lax.fori_loop(0, pairs, two_rows, 0)

    def gather(m, first=False):
        if first:
            even, odd = jnp.float32(EVEN[0]), jnp.float32(ODD[0])
        else:
            even, odd = pick(EVEN, m), pick(ODD, m)

        def one_row(row, sums):
            sums = list(sums)
            for t in range(2):
                for orb in range(4):
                    now = (site(0, orb, t, HALO + row), site(1, orb, t, HALO + row))
                    vr, vi = vel[2 * orb, t, row], vel[2 * orb + 1, t, row]
                    for which, (ur, ui) in enumerate(now):
                        sums[2 * which] += vr * ur + vi * ui
                        sums[2 * which + 1] += vr * ui - vi * ur
                    re = even * now[0][0] - odd * now[1][1]
                    im = even * now[0][1] + odd * now[1][0]
                    if not first:
                        re, im = re + tot[2 * orb, t, row], im + tot[2 * orb + 1, t, row]
                    tot[2 * orb, t, row], tot[2 * orb + 1, t, row] = re, im
            return tuple(sums)

        sums = lax.fori_loop(0, ROWS, one_row, (zero,) * 4)
        for which in range(4):
            mom[4 * m + which] = sums[which]

    step(0, 1, 1, (EXT - 2) // 2, first=True)
    gather(0, first=True)

    def two_steps(m, carry):
        step(1, 0, m, EXT // 2 - m)
        step(0, 1, m + 1, EXT // 2 - 1 - m)
        gather(m)
        return carry

    lax.fori_loop(1, TERMS // 2, two_steps, 0)

    scale = 2.0 / math.sqrt(4.0 * nx * ny)
    local = zero
    for k in range(TERMS):
        re = jnp.sum(mom[2 * k + 1], axis=1, keepdims=True)
        im = -jnp.sum(mom[2 * k], axis=1, keepdims=True)
        local = jnp.where(lane == 2 * k, re, local)
        local = jnp.where(lane == 2 * k + 1, im, local)
    local = local * scale

    def spread(value, msg, slots, me, size, target, send_sem, recv_sem):
        msg[...] = value
        slots[me] = value

        def copy_to(other, slot, d):
            return pltpu.make_async_remote_copy(
                src_ref=msg,
                dst_ref=slots.at[slot],
                send_sem=send_sem.at[d],
                recv_sem=recv_sem.at[slot],
                device_id=target(other),
                device_id_type=MESH,
            )

        def send(d, carry):
            copy_to(lax.rem(me + d, size), me, d).start()
            return carry

        def finish(d, carry):
            other = lax.rem(me + d, size)
            copy_to(other, me, d).wait_send()
            copy_to(other, other, d).wait_recv()
            return carry

        lax.fori_loop(1, size, send, 0)
        return lambda: lax.fori_loop(1, size, finish, 0)

    def total(slots, size):
        value = slots[0]
        for at in range(1, size):
            value = value + slots[at]
        return value

    finish_x = spread(local, msg_x, in_x, gx, gx_size, lambda other: (other, gy), rxs_sem, rxr_sem)

    out_rows = [outv.at[t].reshape(2 * STATES * 4 * ROWS, LANES) for t in range(2)]
    outs = []
    for t in range(2):

        def finish_row(row, carry):
            for orb in range(4):
                v = tot[2 * orb, t, row], tot[2 * orb + 1, t, row]
                if orb != B1:
                    which = phi_of[orb]
                    v = rot_back(gauge[which, 0, t, pl.ds(row, 1), :], gauge[which, 1, t, pl.ds(row, 1), :], v)
                for part in range(2):
                    out_rows[t][pl.ds(part * STATES * 4 * ROWS + orb * ROWS + row, STATES, stride=4 * ROWS), :] = v[part]
            return carry

        lax.fori_loop(0, ROWS, finish_row, 0)
        copy = pltpu.make_async_copy(outv.at[t], evo_h.at[:, :, :, :, pl.ds(t * LANES, LANES)], out_sem.at[t])
        copy.start()
        outs.append(copy)

    finish_x()
    finish_y = spread(total(in_x, gx_size), msg_y, in_y, gy, gy_size, lambda other: (gx, other), rys_sem, ryr_sem)
    finish_y()
    mom_ref[...] = total(in_y, gy_size)
    for copy in outs:
        copy.wait()


def per_device(nx, ny, gx_size, gy_size, angles, bond_flux, coupling):
    f32 = jnp.float32
    tile = (STATES, LANES)
    evolved, moments = pl.pallas_call(
        functools.partial(kernel, nx, ny, gx_size, gy_size),
        out_shape=(
            jax.ShapeDtypeStruct((2, STATES, 4, ROWS, COLS), f32),
            jax.ShapeDtypeStruct(tile, f32),
        ),
        in_specs=[pl.BlockSpec(memory_space=pl.ANY)] * 3,
        out_specs=(pl.BlockSpec(memory_space=pl.ANY), pl.BlockSpec(memory_space=pltpu.VMEM)),
        scratch_shapes=[
            pltpu.VMEM((2, STATES, 4, EXT, LANES), f32),
            pltpu.VMEM((2, 7, EXT, LANES), jnp.int32),
            pltpu.VMEM((TILES, 8 * PAD, LANES), f32),
            pltpu.VMEM((2, 8, TILES, EXT) + tile, f32),
            pltpu.VMEM((13, TILES, EXT, LANES), f32),
            pltpu.VMEM((3, TILES, EXT, LANES), f32),
            pltpu.VMEM((3, 2, 2, ROWS, LANES), f32),
            pltpu.VMEM((TILES, EXT, LANES), f32),
            pltpu.VMEM((8, 2, ROWS) + tile, f32),
            pltpu.VMEM((8, 2, ROWS) + tile, f32),
            pltpu.VMEM((2, 2, STATES, 4, ROWS, LANES), f32),
            pltpu.VMEM((2 * TERMS,) + tile, f32),
            pltpu.VMEM((2, 5) + tile, f32),
            pltpu.VMEM((2, 3, 5) + tile, f32),
            pltpu.VMEM(tile, f32),
            pltpu.VMEM(tile, f32),
            pltpu.VMEM((gx_size,) + tile, f32),
            pltpu.VMEM((gy_size,) + tile, f32),
            pltpu.SemaphoreType.DMA((2, 3)),
            pltpu.SemaphoreType.DMA((2,)),
            pltpu.SemaphoreType.DMA((2, 2, 3)),
            pltpu.SemaphoreType.DMA((2, 2, 3)),
            pltpu.SemaphoreType.DMA((2, 3)),
            pltpu.SemaphoreType.DMA((2, 3)),
            pltpu.SemaphoreType.DMA((gx_size,)),
            pltpu.SemaphoreType.DMA((gx_size,)),
            pltpu.SemaphoreType.DMA((gy_size,)),
            pltpu.SemaphoreType.DMA((gy_size,)),
        ],
        compiler_params=pltpu.CompilerParams(
            collective_id=0, has_side_effects=True, vmem_limit_bytes=48 * 2**20
        ),
        name="evolve",
    )(angles, bond_flux, coupling)
    return evolved, moments[:, : 2 * TERMS].T.reshape(TERMS, 2, STATES)


def solution(mesh):
    in_specs = (P(None, None, "gx", "gy"), P(None, "gx", "gy"), P("gx", "gy"))
    out_specs = (P(None, None, None, "gx", "gy"), P())
    gx_size, gy_size = mesh.shape["gx"], mesh.shape["gy"]
    return jax.shard_map(
        functools.partial(per_device, gx_size * ROWS, gy_size * COLS, gx_size, gy_size),
        mesh=mesh,
        in_specs=in_specs,
        out_specs=out_specs,
        check_vma=False,
    )
```

```python
import functools
import math

import jax
import jax.numpy as jnp
from jax import lax
from jax.experimental import pallas as pl
from jax.experimental.pallas import tpu as pltpu
from jax.sharding import PartitionSpec as P

TERMS = 16
QUANTA = 64
PHASE_SPAN = 12.0

STATES = 8
ROWS = 16
COLS = 256
LANES = 128
HALO = 8
EXT = ROWS + 2 * HALO
PAD = EXT + 8
BLOCKS = EXT // 8
SIDE = 2 * HALO
TILES = 3
DEEP = (COLS + SIDE) // 16
ROW0 = 8
UNROLL = 1
A1, B2, B1, A2 = 0, 1, 2, 3
MESH = pl.DeviceIdType.MESH

T2C, T2S, T4C, T4S, T5C, T5S, CPL = range(7)


def bessel_value(degree, argument):
    running = 0.0
    for number in range(60):
        running += (
            (-1.0) ** number
            * (argument / 2.0) ** (2 * number + degree)
            / (math.factorial(number) * math.factorial(number + degree))
        )
    return running


EVEN = [(1.0 if m == 0 else 2.0) * (-1.0) ** m * bessel_value(2 * m, PHASE_SPAN) for m in range(TERMS // 2)]
ODD = [-2.0 * (-1.0) ** m * bessel_value(2 * m + 1, PHASE_SPAN) for m in range(TERMS // 2)]

SIN_COEF = [(-1.0) ** n * math.pi ** (2 * n + 1) / math.factorial(2 * n + 1) for n in range(6)]
COS_COEF = [(-1.0) ** n * math.pi ** (2 * n) / math.factorial(2 * n) for n in range(7)]


def turn(f):
    r = f - jnp.floor(f + 0.5)
    q = r * r
    s = SIN_COEF[-1]
    for value in reversed(SIN_COEF[:-1]):
        s = s * q + value
    s = s * r
    c = COS_COEF[-1]
    for value in reversed(COS_COEF[:-1]):
        c = c * q + value
    return 1.0 - 2.0 * s * s, 2.0 * s * c


def rot(c, s, v):
    return c * v[0] - s * v[1], s * v[0] + c * v[1]


def rot_back(c, s, v):
    return c * v[0] + s * v[1], c * v[1] - s * v[0]


def add(*pairs):
    re, im = pairs[0]
    for pair in pairs[1:]:
        re, im = re + pair[0], im + pair[1]
    return re, im


def kernel(
    nx, ny, gx_size, gy_size,
    ang_h, flux_h, coup_h, evo_h, mom_ref,
    ang, fli, flf, u, hist, ft, phf, af, px, spread_m, perm_m, back_m, gauge, chi, vel, tf, tl, outv, mom, pack, got, msg_1, msg_2, in_1, in_2,
    load_sem, out_sem, xs_sem, xr_sem, ps_sem, pr_sem, s1_sem, r1_sem, s2_sem, r2_sem,
):
    gx, gy = lax.axis_index("gx"), lax.axis_index("gy")
    group_1, group_2 = gx_size // 2, 2 * gy_size
    half, place_1 = gx // group_1, lax.rem(gx, group_1)
    place_2 = half * gy_size + gy

    def near(dx, dy):
        return (lax.rem(gx + dx + gx_size, gx_size), lax.rem(gy + dy + gy_size, gy_size))

    def peer_1(other):
        return (half * group_1 + other, gy)

    def peer_2(other):
        return (other // gy_size * group_1 + place_1, lax.rem(other, gy_size))

    lane = lax.broadcasted_iota(jnp.int32, (STATES, LANES), 1)
    sub = lax.broadcasted_iota(jnp.int32, (8, LANES), 0)
    first_lane, last_lane = lane == 0, lane == LANES - 1
    zero = jnp.zeros((STATES, LANES), jnp.float32)

    loads = []
    for t in range(2):
        span = pl.ds(t * LANES, LANES)
        own = pl.ds(HALO, ROWS)
        loads.append(pltpu.make_async_copy(flux_h.at[:, :, span], fli.at[t, :, own, :], load_sem.at[t, 0]))
        loads.append(pltpu.make_async_copy(coup_h.at[:, span], flf.at[t, pl.ds(7 * PAD + HALO, ROWS), :], load_sem.at[t, 1]))
        loads.append(pltpu.make_async_copy(ang_h.at[:, :, :, span], ang.at[t, :, :, own, :], load_sem.at[t, 2]))
    for copy in loads:
        copy.start()

    barrier = pltpu.get_barrier_semaphore()

    def greet(peer, me, size):
        def one(d, carry):
            pl.semaphore_signal(barrier, inc=1, device_id=peer(lax.rem(me + d, size)), device_id_type=MESH)
            return carry

        lax.fori_loop(1, size, one, 0)

    for dx in (-1, 0, 1):
        for dy in (-1, 0, 1):
            if dx or dy:
                pl.semaphore_signal(barrier, inc=1, device_id=near(dx, dy), device_id_type=MESH)
    greet(peer_1, place_1, group_1)
    greet(peer_2, place_2, group_2)

    for t in range(TILES):
        for plane in range(8):
            flf[t, pl.ds(plane * PAD + EXT, 8), :] = zero

    for copy in loads:
        copy.wait()

    def flux_to_float(t, start, count):
        for plane in range(7):
            flf[t, pl.ds(plane * PAD + start, count), :] = fli[t, plane, pl.ds(start, count), :].astype(jnp.float32)

    for t in range(2):
        flux_to_float(t, HALO, ROWS)

    group = lane // HALO

    def packed(side, value_of):
        out = zero
        for r in range(8):
            value = value_of(r)
            move = (SIDE * r + (SIDE if side == 0 else 0)) % LANES
            if move:
                value = pltpu.roll(value, move, 1)
            out = jnp.where(group == 2 * r + 1 - side, value, out)
        return out

    def pack_angles(orb, carry):
        for side in range(2):
            for block in range(2):
                rows = pl.ds(HALO + 8 * block, 8)
                pack[side, block, orb] = packed(side, lambda r: ang[1 - side, r, orb, rows, :])
        return carry

    lax.fori_loop(0, 4, pack_angles, 0)
    for side in range(2):
        for block in range(2):
            pack[side, block, 4] = packed(side, lambda r: flf[1 - side, pl.ds(r * PAD + HALO + 8 * block, 8), :])

    pl.semaphore_wait(barrier, 8 + group_1 - 1 + group_2 - 1)

    row_copies = []
    for side, dx in ((0, 1), (1, -1)):
        src_rows = pl.ds(ROWS - HALO, HALO) if side == 0 else pl.ds(0, HALO)
        low = 0 if side == 0 else HALO + ROWS
        for t in range(2):
            span = pl.ds(t * LANES, LANES)
            for what, (src, dst) in enumerate(
                (
                    (flux_h.at[:, src_rows, span], fli.at[t, :, pl.ds(low, HALO), :]),
                    (coup_h.at[src_rows, span], flf.at[t, pl.ds(7 * PAD + low, HALO), :]),
                    (ang_h.at[:, :, src_rows, span], ang.at[t, :, :, pl.ds(low, HALO), :]),
                )
            ):
                row_copies.append(
                    (
                        what,
                        pltpu.make_async_remote_copy(
                            src_ref=src,
                            dst_ref=dst,
                            send_sem=xs_sem.at[side, t, what],
                            recv_sem=xr_sem.at[side, t, what],
                            device_id=near(dx, 0),
                            device_id_type=MESH,
                        ),
                    )
                )
    pack_copies = []
    for side, dy in ((0, 1), (1, -1)):
        for dx, src, dst in (
            (0, pack.at[side], got.at[side, pl.ds(1, 2)]),
            (1, pack.at[side, 1], got.at[side, 0]),
            (-1, pack.at[side, 0], got.at[side, 3]),
        ):
            pack_copies.append(
                pltpu.make_async_remote_copy(
                    src_ref=src,
                    dst_ref=dst,
                    send_sem=ps_sem.at[side, 1 - dx],
                    recv_sem=pr_sem.at[side, 1 - dx],
                    device_id=near(dx, dy),
                    device_id_type=MESH,
                )
            )
    for what, copy in row_copies:
        if what < 2:
            copy.start()
    for copy in pack_copies:
        copy.start()
    for what, copy in row_copies:
        if what == 2:
            copy.start()

    def flux_of(t, plane, start, count=8):
        return flf[t, pl.ds(plane * PAD + start, count), :]

    def wrapped(value):
        return value - QUANTA * jnp.floor(value * (1.0 / QUANTA))

    def cell_phases(t, start, carry):
        if start < HALO:
            run = flux_of(t, 1, start + 1) - flux_of(t, 0, start + 1)
            for reach in (1, 2, 4):
                run = run + jnp.where(sub < 8 - reach, pltpu.roll(run, 8 - reach, 0), 0.0)
        else:
            run = flux_of(t, 0, start) - flux_of(t, 1, start)
            if start == HALO:
                run = jnp.where(sub == 0, 0.0, run)
            for reach in (1, 2, 4):
                run = run + jnp.where(sub >= reach, pltpu.roll(run, reach, 0), 0.0)
            if carry is not None:
                run = run + carry
        run = wrapped(run)
        chi[t, pl.ds(start, 8), :] = run
        th0, th3, th6 = (flux_of(t, plane, start) for plane in (0, 3, 6))
        rows = pl.ds(start, 8)
        span = pl.ds(t * LANES, LANES)
        px[A1, rows, span] = wrapped(run - th0 + QUANTA // 2)
        px[B2, rows, span] = wrapped(th6 + th3 + run + QUANTA // 2)
        px[B1, rows, span] = run
        px[A2, rows, span] = wrapped(th6 + run)
        return jnp.broadcast_to(run[7:8, :], (8, LANES))

    carries = []
    for t in range(2):
        carry = None
        for start in (HALO, HALO + 8):
            carry = cell_phases(t, start, carry)
            for orb in range(4):
                c, s = turn(px[orb, pl.ds(start, 8), pl.ds(t * LANES, LANES)] * (1.0 / QUANTA))
                if orb in (A1, A2):
                    c, s = 0.5 * c, 0.5 * s
                gauge[orb, 0, t, pl.ds(start - HALO, 8), :] = c
                gauge[orb, 1, t, pl.ds(start - HALO, 8), :] = s
        carries.append(carry)

    def row_place(shape):
        at = lax.broadcasted_iota(jnp.int32, shape, 0)
        return jnp.where(at < COLS + HALO, at + HALO, jnp.where(at < COLS + SIDE, at - COLS - HALO, -1))

    def one_hot(here):
        return jnp.where(here, 1.0, 0.0).astype(jnp.bfloat16)

    at_row = row_place((TILES * LANES, LANES))
    at_lane = lax.rem(lax.broadcasted_iota(jnp.int32, (TILES * LANES, LANES), 1), SIDE) * DEEP

    def make_spread(y, carry):
        spread_m[:, pl.ds(pl.multiple_of(y * LANES, LANES), LANES)] = one_hot(at_row == at_lane + y)
        return carry

    lax.fori_loop(0, DEEP, make_spread, 0)
    wide = lax.broadcasted_iota(jnp.int32, (COLS, TILES * LANES), 1)
    tall = lax.broadcasted_iota(jnp.int32, (COLS, TILES * LANES), 0)
    perm_m[...] = one_hot((tall + HALO == lax.rem(wide, SIDE) * DEEP + wide // SIDE) & (wide < SIDE * DEEP))
    wide = lax.broadcasted_iota(jnp.int32, (TILES * LANES, COLS), 1)
    tall = lax.broadcasted_iota(jnp.int32, (TILES * LANES, COLS), 0)
    back_m[...] = one_hot((wide + HALO == lax.rem(tall, SIDE) * DEEP + tall // SIDE) & (tall < SIDE * DEEP))

    def moved(value, matrix):
        parts = []
        for _ in range(3):
            parts.append(value.astype(jnp.bfloat16))
            value = value - parts[-1].astype(jnp.float32)
        out = jnp.dot(jnp.concatenate(parts, axis=0), matrix, preferred_element_type=jnp.float32)
        size = value.shape[0]
        return out[:size] + out[size : 2 * size] + out[2 * size :]

    lane_group = lane // SIDE

    def exchanged(values):
        values = list(values)
        for s in (1, 2, 4):
            keep = (lane_group // s) % 2 == 0
            for i in range(8):
                if not i & s:
                    one, two = values[i], values[i | s]
                    values[i] = jnp.where(keep, one, pltpu.roll(two, SIDE * s, 1))
                    values[i | s] = jnp.where(keep, pltpu.roll(one, LANES - SIDE * s, 1), two)
        return values

    def spread_angles(blocks):
        def spread_orb(orb, carry):
            value = jnp.concatenate(
                [
                    jnp.concatenate(
                        [ang[t, :, orb, pl.ds(8 * block, 8), :].reshape(STATES * 8, LANES) for t in range(2)], axis=1
                    )
                    for block in blocks
                ],
                axis=0,
            )
            out = moved(value, perm_m[...])
            for which, block in enumerate(blocks):
                parts = [
                    [
                        out[64 * which + 8 * r : 64 * which + 8 * r + 8, LANES * t : LANES * t + LANES]
                        for r in range(8)
                    ]
                    for t in range(TILES)
                ]
                deep = exchanged(parts[0]) + exchanged(parts[1])
                last = parts[2][0]
                for r in range(1, 8):
                    last = jnp.where(lane_group == r, pltpu.roll(parts[2][r], SIDE * r, 1), last)
                for y, value in enumerate(deep + [last]):
                    af[orb, y, pl.ds(8 * block, 8), :] = value
            return carry

        lax.fori_loop(0, 4, spread_orb, 0)

    spread_angles((1, 2))

    for what, copy in row_copies:
        if what < 2:
            copy.wait()
    for t in range(2):
        for start in (0, HALO + ROWS):
            flux_to_float(t, start, HALO)
            cell_phases(t, start, carries[t])
    for copy in pack_copies:
        copy.wait()

    beside = lax.rem(lane, SIDE)

    def unpack(what, block):
        return jnp.where(beside < HALO, got[1, block, what], got[0, block, what])

    for block in range(BLOCKS):
        values = unpack(4, block)
        for which in range(8):
            move = (LANES - SIDE * which) % LANES
            flf[2, pl.ds(which * PAD + 8 * block, 8), :] = pltpu.roll(values, move, 1) if move else values
    carry = None
    for start in (HALO, HALO + 8, HALO + ROWS, 0):
        carry = cell_phases(2, start, carry)

    def right(values):
        rolled = [pltpu.roll(value, 1, 1) for value in values]
        edges = [pltpu.roll(values[2], LANES - SIDE + 1, 1), rolled[0], rolled[1]]
        return [jnp.where(first_lane, edges[t], rolled[t]) for t in range(TILES)]

    def left(values):
        rolled = [pltpu.roll(value, LANES - 1, 1) for value in values]
        edge = pltpu.roll(values[0], SIDE - 1, 1)
        return [
            jnp.where(last_lane, rolled[1], rolled[0]),
            jnp.where(last_lane, rolled[2], rolled[1]),
            jnp.where(lane == SIDE - 1, edge, rolled[2]),
        ]

    for start in range(0, EXT, 8):
        rows = pl.ds(start, 8)
        th = [[flux_of(t, plane, start) for plane in range(8)] for t in range(TILES)]
        cell = [chi[t, rows, :] for t in range(TILES)]
        cell_left, cell_right = right(cell), left(cell)
        far = left([th[t][6] + th[t][3] for t in range(TILES)])
        for t in range(TILES):
            span = pl.ds(t * LANES, LANES)
            below = [flux_of(t, plane, start + 1) for plane in (6, 3, 1, 0)]
            px[4, rows, span] = wrapped(th[t][2] - th[t][0] + cell[t] - cell_left[t])
            px[5, rows, span] = wrapped(th[t][4] + th[t][6] - below[0] - below[1] + below[2] - below[3])
            px[6, rows, span] = wrapped(th[t][5] + th[t][6] - far[t] + cell[t] - cell_right[t])
            rest = th[t][7]
            for part in range(3):
                head = rest.astype(jnp.bfloat16).astype(jnp.float32)
                px[7 + part, rows, span] = head
                rest = rest - head

    planes = px[...].reshape(10 * EXT, TILES * LANES).astype(jnp.bfloat16)
    lane_place = lax.rem(lane, SIDE) * DEEP
    sub_i = gx * ROWS - HALO + sub

    def cell_inside(y, block):
        j = gy * COLS - HALO + lane_place + y
        i = sub_i + 8 * block
        return (j >= 0) & (j < ny) & (i >= 0) & (i < nx)

    def make_tables(y, carry):
        out = jnp.dot(
            planes,
            spread_m[:, pl.ds(pl.multiple_of(y * LANES, LANES), LANES)],
            preferred_element_type=jnp.float32,
        )
        place = lane_place + y
        j = gy * COLS - HALO + place
        for block in range(BLOCKS):
            rows = pl.ds(ROW0 + 8 * block, 8)
            part = [out[which * EXT + 8 * block : which * EXT + 8 * block + 8, :] for which in range(10)]
            for orb in range(4):
                phf[orb, y, pl.ds(8 * block, 8), :] = part[orb] * (1.0 / QUANTA)
            here = cell_inside(y, block)
            for which, good in (
                (T2C, here & (j >= 1) & (place >= 1)),
                (T4C, here & (sub_i + 8 * block + 1 < nx)),
                (T5C, here & (j + 1 < ny) & (place < SIDE * DEEP - 1)),
            ):
                c, s = turn(part[4 + which // 2] * (1.0 / QUANTA))
                ft[which, y + 1, rows, :] = jnp.where(good, c, 0.0)
                ft[which + 1, y + 1, rows, :] = jnp.where(good, s, 0.0)
            ft[CPL, y + 1, rows, :] = jnp.where(here, part[7] + part[8] + part[9], 0.0)
        return carry

    lax.fori_loop(0, DEEP, make_tables, 0)
    for block in range(BLOCKS):
        rows = pl.ds(ROW0 + 8 * block, 8)
        for which in (T2C, T2S):
            ft[which, DEEP + 1, rows, :] = pltpu.roll(ft[which, 1, rows, :], LANES - 1, 1)
        for which in (T5C, T5S):
            ft[which, 0, rows, :] = pltpu.roll(ft[which, DEEP, rows, :], 1, 1)

    def start_values(blocks):
        def start_one(y, carry):
            place = lane_place + y
            beyond = (place < HALO) | (place >= COLS + HALO)
            move = jnp.where(y <= HALO, LANES - HALO - y, SIDE + HALO - y)
            for block in blocks:
                here = cell_inside(y, block)
                rows = pl.ds(8 * block, 8)
                for orb in range(4):
                    angle = jnp.where(beyond, pltpu.roll(unpack(orb, block), move, 1), af[orb, y, rows, :])
                    c, s = turn(angle * (0.5 / math.pi) + phf[orb, y, rows, :])
                    size = 2.0 if orb in (A1, A2) else 1.0
                    u[0, 2 * orb, y + 1, pl.ds(ROW0 + 8 * block, 8), :] = jnp.where(here, size * c, 0.0)
                    u[0, 2 * orb + 1, y + 1, pl.ds(ROW0 + 8 * block, 8), :] = jnp.where(here, size * s, 0.0)
            return carry

        lax.fori_loop(0, DEEP, start_one, 0)

    start_values((1, 2))
    for what, copy in row_copies:
        if what == 2:
            copy.wait()
    spread_angles((0, 3))
    start_values((0, 3))

    def site(buf, orb, y, row):
        rows = pl.ds(ROW0 + row, 8)
        return u[buf, 2 * orb, y + 1, rows, :], u[buf, 2 * orb + 1, y + 1, rows, :]

    def table(which, y, row):
        rows = pl.ds(ROW0 + row, 8)
        return ft[which, y + 1, rows, :], ft[which + 1, y + 1, rows, :]

    def join(buf, row):
        rows = pl.ds(ROW0 + row, 8)
        for part in range(2):
            for orb in (B1, A2):
                u[buf, 2 * orb + part, 0, rows, :] = pltpu.roll(u[buf, 2 * orb + part, DEEP, rows, :], 1, 1)
            for orb in (A1, B2):
                u[buf, 2 * orb + part, DEEP + 1, rows, :] = pltpu.roll(u[buf, 2 * orb + part, 1, rows, :], LANES - 1, 1)

    for block in range(BLOCKS):
        join(0, 8 * block)

    def velocity(y, carry):
        place = lane_place + y
        own = jnp.where((place >= HALO) & (place < COLS + HALO), 0.5, 0.0)
        for block in range(2):
            row = HALO + 8 * block
            v = [None] * 4
            v[A1] = [own * part for part in site(0, B1, y, row - 1)]
            v[B1] = [-own * part for part in site(0, A1, y, row + 1)]
            v[A2] = [-own * part for part in rot(*table(T4C, y, row), site(0, B2, y, row + 1))]
            v[B2] = [own * part for part in rot_back(*table(T4C, y, row - 1), site(0, A2, y, row - 1))]
            for orb in range(4):
                for part in range(2):
                    vel[y, block, 2 * orb + part] = v[orb][part]
        return carry

    lax.fori_loop(0, DEEP, velocity, 0)

    def step_at(src, dst, y, row, first):
        a1, b2, b1, a2 = (site(src, orb, y, row) for orb in range(4))
        hop = ft[CPL, y + 1, pl.ds(ROW0 + row, 8), :]
        new = [None] * 4
        new[A1] = add(b1, site(src, B1, y, row - 1), rot(*table(T2C, y, row), site(src, B1, y - 1, row)))
        new[B1] = add(
            a1,
            site(src, A1, y, row + 1),
            rot_back(*table(T2C, y + 1, row), site(src, A1, y + 1, row)),
            (hop * a2[0], hop * a2[1]),
        )
        new[A2] = add(
            b2,
            rot(*table(T4C, y, row), site(src, B2, y, row + 1)),
            rot(*table(T5C, y, row), site(src, B2, y + 1, row)),
            (hop * b1[0], hop * b1[1]),
        )
        new[B2] = add(
            a2,
            rot_back(*table(T4C, y, row - 1), site(src, A2, y, row - 1)),
            rot_back(*table(T5C, y - 1, row), site(src, A2, y - 1, row)),
        )
        for orb in range(4):
            size = 1.0 if orb in (A1, A2) else 0.25
            for part in range(2):
                value = new[orb][part]
                rows = pl.ds(ROW0 + row, 8)
                if first:
                    value = (0.5 * size) * value
                else:
                    value = (value if size == 1.0 else size * value) - u[dst, 2 * orb + part, y + 1, rows, :]
                u[dst, 2 * orb + part, y + 1, rows, :] = value

    def step(src, dst, rows, first=False):
        def step_one(y, carry):
            for row in rows:
                step_at(src, dst, y, row, first)
            return carry

        lax.fori_loop(0, DEEP, step_one, 0, unroll=UNROLL)
        for row in rows:
            join(dst, row)

        @pl.when(gx == 0)
        def _():
            for orb in (B1, A2):
                for part in range(2):
                    u[dst, 2 * orb + part, :, pl.ds(ROW0 + HALO - 1, 1), :] = jnp.zeros((DEEP + 2, 1, LANES), jnp.float32)

        @pl.when(gx == gx_size - 1)
        def _():
            for orb in (A1, B2):
                for part in range(2):
                    u[dst, 2 * orb + part, :, pl.ds(ROW0 + HALO + ROWS, 1), :] = jnp.zeros((DEEP + 2, 1, LANES), jnp.float32)

    def gather(k):
        def gather_one(y, sums):
            sums = list(sums)
            for block in range(2):
                for orb in range(4):
                    vr, vi = vel[y, block, 2 * orb], vel[y, block, 2 * orb + 1]
                    for which in range(2):
                        ur, ui = site(which, orb, y, HALO + 8 * block)
                        hist[k + which, y, block, 2 * orb], hist[k + which, y, block, 2 * orb + 1] = ur, ui
                        sums[2 * which] += vr * ur + vi * ui
                        sums[2 * which + 1] += vr * ui - vi * ur
            return tuple(sums)

        sums = lax.fori_loop(0, DEEP, gather_one, (zero,) * 4)
        for which in range(4):
            mom[2 * k + which] = sums[which]

    far_rows, mid_rows, own_rows = (0, 8, 16, 24), (4, 12, 20), (8, 16)
    step(0, 1, far_rows, first=True)
    gather(0)

    def early(m, carry):
        step(1, 0, far_rows)
        step(0, 1, far_rows)
        gather(2 * m)
        return carry

    def late(m, carry):
        step(1, 0, mid_rows)
        step(0, 1, mid_rows)
        gather(2 * m)
        return carry

    lax.fori_loop(1, 4, early, 0)
    lax.fori_loop(4, TERMS // 2 - 1, late, 0)
    step(1, 0, mid_rows)
    step(0, 1, own_rows)
    gather(TERMS - 2)

    sums = []
    for part in (1, 0):
        for k in range(TERMS):
            sums.append(jnp.sum(mom[2 * k + part], axis=0, keepdims=True))
    state = lax.broadcasted_iota(jnp.int32, (STATES, LANES), 0)
    ones = jnp.where(lane_group == state, 1.0, 0.0)
    local = lax.dot_general(
        ones,
        jnp.concatenate(sums + [jnp.zeros((LANES - 2 * TERMS, LANES), jnp.float32)], axis=0),
        (((1,), (1,)), ((), ())),
        precision=lax.Precision.HIGHEST,
        preferred_element_type=jnp.float32,
    )
    local = jnp.where(lane < TERMS, local, -local) * (1.0 / math.sqrt(4.0 * nx * ny))
    wide = 2 * TERMS
    spread_out = zero
    for q in range(4):
        value = pltpu.roll(local, wide * q, 1) if q else local
        spread_out = jnp.where((lax.rem(sub, 4) == q) & (lane // wide == q), value, spread_out)
    folded = jnp.concatenate(
        [jnp.sum(spread_out[:4], axis=0, keepdims=True), jnp.sum(spread_out[4:], axis=0, keepdims=True)], axis=0
    )

    def spread(value, msg, slots, me, size, peer, send_sem, recv_sem):
        msg[...] = value
        slots[me] = value

        def copy_to(other, slot, d):
            return pltpu.make_async_remote_copy(
                src_ref=msg,
                dst_ref=slots.at[slot],
                send_sem=send_sem.at[d],
                recv_sem=recv_sem.at[slot],
                device_id=peer(other),
                device_id_type=MESH,
            )

        def send(d, carry):
            copy_to(lax.rem(me + d, size), me, d).start()
            return carry

        def finish(d, carry):
            other = lax.rem(me + d, size)
            copy_to(other, me, d).wait_send()
            copy_to(other, other, d).wait_recv()
            return carry

        lax.fori_loop(1, size, send, 0)
        return lambda: lax.fori_loop(1, size, finish, 0)

    def total(slots, size):
        value = slots[0]
        for at in range(1, size):
            value = value + slots[at]
        return value

    def out_copy(orb):
        return pltpu.make_async_copy(outv.at[:, :, orb], evo_h.at[:, :, orb], out_sem.at[orb])

    def evolve(orb, carry):
        def evolve_one(y, carry):
            for block in range(2):
                re, im = zero, zero
                for m in range(TERMS // 2):
                    a, b = ((hist[2 * m + n, y, block, 2 * orb], hist[2 * m + n, y, block, 2 * orb + 1]) for n in range(2))
                    re = re + (EVEN[m] * a[0] - ODD[m] * b[1])
                    im = im + (EVEN[m] * a[1] + ODD[m] * b[0])
                tf[block, y], tf[2 + block, y] = re, im
            return carry

        lax.fori_loop(0, DEEP, evolve_one, 0)

        def back(which, carry):
            tiles = [exchanged([tf[which, 8 * t + i] for i in range(8)]) for t in range(2)]
            last = tf[which, DEEP - 1]
            tiles.append([pltpu.roll(last, LANES - SIDE * r, 1) if r else last for r in range(8)])
            for t in range(TILES):
                for r in range(8):
                    tl[which, pl.ds(8 * r, 8), pl.ds(LANES * t, LANES)] = tiles[t][r]
            return carry

        lax.fori_loop(0, 4, back, 0)
        out = moved(tl[...].reshape(4 * 64, TILES * LANES), back_m[...])
        for block in range(2):
            rows = pl.ds(8 * block, 8)
            c = jnp.concatenate([gauge[orb, 0, t, rows, :] for t in range(2)], axis=1)
            s = jnp.concatenate([gauge[orb, 1, t, rows, :] for t in range(2)], axis=1)
            for r in range(8):
                at = 64 * block + 8 * r
                v = rot_back(c, s, (out[at : at + 8, :], out[128 + at : 128 + at + 8, :]))
                outv[0, r, orb, rows, :], outv[1, r, orb, rows, :] = v
        out_copy(orb).start()
        return carry

    finish_1 = spread(folded, msg_1, in_1, place_1, group_1, peer_1, s1_sem, r1_sem)
    lax.fori_loop(0, 2, evolve, 0)
    finish_1()
    finish_2 = spread(total(in_1, group_1), msg_2, in_2, place_2, group_2, peer_2, s2_sem, r2_sem)
    lax.fori_loop(2, 4, evolve, 0)
    finish_2()
    folded = total(in_2, group_2)
    rows = jnp.where(sub < 4, folded[0:1, :], folded[1:2, :])
    result = rows
    for q in range(1, 4):
        result = jnp.where(lax.rem(sub, 4) == q, pltpu.roll(rows, LANES - wide * q, 1), result)
    mom_ref[0] = result[:, :TERMS]
    mom_ref[1] = pltpu.roll(result, LANES - TERMS, 1)[:, :TERMS]
    for orb in range(4):
        out_copy(orb).wait()


def per_device(nx, ny, gx_size, gy_size, angles, bond_flux, coupling):
    f32 = jnp.float32
    tile = (STATES, LANES)
    group_1, group_2 = gx_size // 2, 2 * gy_size
    evolved, moments = pl.pallas_call(
        functools.partial(kernel, nx, ny, gx_size, gy_size),
        out_shape=(
            jax.ShapeDtypeStruct((2, STATES, 4, ROWS, COLS), f32),
            jax.ShapeDtypeStruct((2, STATES, TERMS), f32),
        ),
        in_specs=[pl.BlockSpec(memory_space=pl.ANY)] * 3,
        out_specs=(pl.BlockSpec(memory_space=pl.ANY), pl.BlockSpec(memory_space=pltpu.VMEM)),
        scratch_shapes=[
            pltpu.VMEM((2, STATES, 4, EXT, LANES), f32),
            pltpu.VMEM((2, 7, EXT, LANES), jnp.int32),
            pltpu.VMEM((TILES, 8 * PAD, LANES), f32),
            pltpu.VMEM((2, 8, DEEP + 2, EXT + 2 * ROW0, LANES), f32),
            pltpu.VMEM((TERMS, DEEP, 2, 8) + tile, f32),
            pltpu.VMEM((7, DEEP + 2, EXT + 2 * ROW0, LANES), f32),
            pltpu.VMEM((4, DEEP, EXT, LANES), f32),
            pltpu.VMEM((4, DEEP, EXT, LANES), f32),
            pltpu.VMEM((10, EXT, TILES * LANES), f32),
            pltpu.VMEM((TILES * LANES, DEEP * LANES), jnp.bfloat16),
            pltpu.VMEM((COLS, TILES * LANES), jnp.bfloat16),
            pltpu.VMEM((TILES * LANES, COLS), jnp.bfloat16),
            pltpu.VMEM((4, 2, 2, ROWS, LANES), f32),
            pltpu.VMEM((TILES, EXT, LANES), f32),
            pltpu.VMEM((DEEP, 2, 8) + tile, f32),
            pltpu.VMEM((4, DEEP) + tile, f32),
            pltpu.VMEM((4, 64, TILES * LANES), f32),
            pltpu.VMEM((2, STATES, 4, ROWS, COLS), f32),
            pltpu.VMEM((2 * TERMS,) + tile, f32),
            pltpu.VMEM((2, 2, 5) + tile, f32),
            pltpu.VMEM((2, BLOCKS, 5) + tile, f32),
            pltpu.VMEM((2, LANES), f32),
            pltpu.VMEM((2, LANES), f32),
            pltpu.VMEM((group_1, 2, LANES), f32),
            pltpu.VMEM((group_2, 2, LANES), f32),
            pltpu.SemaphoreType.DMA((2, 3)),
            pltpu.SemaphoreType.DMA((4,)),
            pltpu.SemaphoreType.DMA((2, 2, 3)),
            pltpu.SemaphoreType.DMA((2, 2, 3)),
            pltpu.SemaphoreType.DMA((2, 3)),
            pltpu.SemaphoreType.DMA((2, 3)),
            pltpu.SemaphoreType.DMA((group_1,)),
            pltpu.SemaphoreType.DMA((group_1,)),
            pltpu.SemaphoreType.DMA((group_2,)),
            pltpu.SemaphoreType.DMA((group_2,)),
        ],
        compiler_params=pltpu.CompilerParams(
            collective_id=0, has_side_effects=True, vmem_limit_bytes=60 * 2**20
        ),
        name="evolve",
    )(angles, bond_flux, coupling)
    return evolved, jnp.transpose(moments, (2, 0, 1))


def solution(mesh):
    in_specs = (P(None, None, "gx", "gy"), P(None, "gx", "gy"), P("gx", "gy"))
    out_specs = (P(None, None, None, "gx", "gy"), P())
    gx_size, gy_size = mesh.shape["gx"], mesh.shape["gy"]
    return jax.shard_map(
        functools.partial(per_device, gx_size * ROWS, gy_size * COLS, gx_size, gy_size),
        mesh=mesh,
        in_specs=in_specs,
        out_specs=out_specs,
        check_vma=False,
    )
```

```python
import functools
import math

import jax
import jax.numpy as jnp
import numpy as np
from jax import lax
from jax.experimental import pallas as pl
from jax.experimental.pallas import tpu as pltpu
from jax.sharding import PartitionSpec as P

TERMS = 16
QUANTA = 64
PHASE_SPAN = 12.0

STATES = 8
ROWS = 16
COLS = 256
LANES = 128
HALO = 8
EXT = ROWS + 2 * HALO
PAD = EXT + 8
BLOCKS = EXT // 8
SIDE = 2 * HALO
TILES = 3
DEEP = (COLS + SIDE) // 16
ROW0 = 8
UNROLL = 1
A1, B2, B1, A2 = 0, 1, 2, 3
MESH = pl.DeviceIdType.MESH

T2C, T2S, T4C, T4S, T5C, T5S, CPL = range(7)


def bessel_value(degree, argument):
    running = 0.0
    for number in range(60):
        running += (
            (-1.0) ** number
            * (argument / 2.0) ** (2 * number + degree)
            / (math.factorial(number) * math.factorial(number + degree))
        )
    return running


EVEN = [(1.0 if m == 0 else 2.0) * (-1.0) ** m * bessel_value(2 * m, PHASE_SPAN) for m in range(TERMS // 2)]
ODD = [-2.0 * (-1.0) ** m * bessel_value(2 * m + 1, PHASE_SPAN) for m in range(TERMS // 2)]

def fitted(function, terms):
    nodes = 0.125 - 0.125 * np.cos(math.pi * (np.arange(40) + 0.5) / 40)
    fit = np.polynomial.chebyshev.Chebyshev.fit(nodes, function(np.sqrt(nodes)), terms - 1, domain=[0.0, 0.25])
    return [float(value) for value in fit.convert(kind=np.polynomial.Polynomial).coef]


SIN_COEF = fitted(lambda r: np.sin(math.pi * r) / r, 5)
COS_COEF = fitted(lambda r: np.cos(math.pi * r), 6)


def small_turn(p, unit=1, size=1.0):
    q = p * p
    s, c = SIN_COEF[-1] / unit ** (2 * len(SIN_COEF) - 1), COS_COEF[-1] / unit ** (2 * len(COS_COEF) - 2)
    for power in reversed(range(len(SIN_COEF) - 1)):
        s = s * q + SIN_COEF[power] / unit ** (2 * power + 1)
    for power in reversed(range(len(COS_COEF) - 1)):
        c = c * q + COS_COEF[power] / unit ** (2 * power)
    s = s * p
    twice = (2.0 * size) * s
    return size - twice * s, twice * c


def turn(f, size=1.0):
    return small_turn(f - jnp.floor(f + 0.5), 1, size)


def rot(c, s, v):
    return c * v[0] - s * v[1], s * v[0] + c * v[1]


def rot_back(c, s, v):
    return c * v[0] + s * v[1], c * v[1] - s * v[0]


def add(*pairs):
    re, im = pairs[0]
    for pair in pairs[1:]:
        re, im = re + pair[0], im + pair[1]
    return re, im


def kernel(
    nx, ny, gx_size, gy_size,
    ang_h, flux_h, coup_h, evo_h, mom_ref,
    ang, fli, flf, u, hist, ft, phf, af, px, spread_m, perm_m, back_m, gauge, chi, vel, tf, tl, outv, mom, pack, got, msg_1, msg_2, in_1, in_2,
    load_sem, out_sem, xs_sem, xr_sem, ps_sem, pr_sem, s1_sem, r1_sem, s2_sem, r2_sem,
):
    gx, gy = lax.axis_index("gx"), lax.axis_index("gy")
    group_1, group_2 = gx_size // 2, 2 * gy_size
    half, place_1 = gx // group_1, lax.rem(gx, group_1)
    place_2 = half * gy_size + gy

    def near(dx, dy):
        return (lax.rem(gx + dx + gx_size, gx_size), lax.rem(gy + dy + gy_size, gy_size))

    def peer_1(other):
        return (half * group_1 + other, gy)

    def peer_2(other):
        return (other // gy_size * group_1 + place_1, lax.rem(other, gy_size))

    lane = lax.broadcasted_iota(jnp.int32, (STATES, LANES), 1)
    sub = lax.broadcasted_iota(jnp.int32, (8, LANES), 0)
    first_lane, last_lane = lane == 0, lane == LANES - 1
    zero = jnp.zeros((STATES, LANES), jnp.float32)

    loads = []
    for t in range(2):
        span = pl.ds(t * LANES, LANES)
        own = pl.ds(HALO, ROWS)
        loads.append(pltpu.make_async_copy(flux_h.at[:, :, span], fli.at[t, :, own, :], load_sem.at[t, 0]))
        loads.append(pltpu.make_async_copy(coup_h.at[:, span], flf.at[t, pl.ds(7 * PAD + HALO, ROWS), :], load_sem.at[t, 1]))
        loads.append(pltpu.make_async_copy(ang_h.at[:, :, :, span], ang.at[t, :, :, own, :], load_sem.at[t, 2]))
    for copy in loads:
        copy.start()

    barrier = pltpu.get_barrier_semaphore()

    def greet(peer, me, size):
        def one(d, carry):
            pl.semaphore_signal(barrier, inc=1, device_id=peer(lax.rem(me + d, size)), device_id_type=MESH)
            return carry

        lax.fori_loop(1, size, one, 0)

    for dx in (-1, 0, 1):
        for dy in (-1, 0, 1):
            if dx or dy:
                pl.semaphore_signal(barrier, inc=1, device_id=near(dx, dy), device_id_type=MESH)
    greet(peer_1, place_1, group_1)
    greet(peer_2, place_2, group_2)

    for t in range(TILES):
        for plane in range(8):
            flf[t, pl.ds(plane * PAD + EXT, 8), :] = zero

    for copy in loads:
        copy.wait()

    def flux_to_float(t, start, count):
        for plane in range(7):
            flf[t, pl.ds(plane * PAD + start, count), :] = fli[t, plane, pl.ds(start, count), :].astype(jnp.float32)

    for t in range(2):
        flux_to_float(t, HALO, ROWS)

    group = lane // HALO

    def packed(side, value_of):
        out = zero
        for r in range(8):
            value = value_of(r)
            move = (SIDE * r + (SIDE if side == 0 else 0)) % LANES
            if move:
                value = pltpu.roll(value, move, 1)
            out = jnp.where(group == 2 * r + 1 - side, value, out)
        return out

    def pack_angles(orb, carry):
        for side in range(2):
            for block in range(2):
                rows = pl.ds(HALO + 8 * block, 8)
                pack[side, block, orb] = packed(side, lambda r: ang[1 - side, r, orb, rows, :])
        return carry

    lax.fori_loop(0, 4, pack_angles, 0)
    for side in range(2):
        for block in range(2):
            pack[side, block, 4] = packed(side, lambda r: flf[1 - side, pl.ds(r * PAD + HALO + 8 * block, 8), :])

    pl.semaphore_wait(barrier, 8 + group_1 - 1 + group_2 - 1)

    row_copies = []
    for side, dx in ((0, 1), (1, -1)):
        src_rows = pl.ds(ROWS - HALO, HALO) if side == 0 else pl.ds(0, HALO)
        low = 0 if side == 0 else HALO + ROWS
        for t in range(2):
            span = pl.ds(t * LANES, LANES)
            for what, (src, dst) in enumerate(
                (
                    (flux_h.at[:, src_rows, span], fli.at[t, :, pl.ds(low, HALO), :]),
                    (coup_h.at[src_rows, span], flf.at[t, pl.ds(7 * PAD + low, HALO), :]),
                    (ang_h.at[:, :, src_rows, span], ang.at[t, :, :, pl.ds(low, HALO), :]),
                )
            ):
                row_copies.append(
                    (
                        what,
                        pltpu.make_async_remote_copy(
                            src_ref=src,
                            dst_ref=dst,
                            send_sem=xs_sem.at[side, t, what],
                            recv_sem=xr_sem.at[side, t, what],
                            device_id=near(dx, 0),
                            device_id_type=MESH,
                        ),
                    )
                )
    pack_copies = []
    for side, dy in ((0, 1), (1, -1)):
        for dx, src, dst in (
            (0, pack.at[side], got.at[side, pl.ds(1, 2)]),
            (1, pack.at[side, 1], got.at[side, 0]),
            (-1, pack.at[side, 0], got.at[side, 3]),
        ):
            pack_copies.append(
                pltpu.make_async_remote_copy(
                    src_ref=src,
                    dst_ref=dst,
                    send_sem=ps_sem.at[side, 1 - dx],
                    recv_sem=pr_sem.at[side, 1 - dx],
                    device_id=near(dx, dy),
                    device_id_type=MESH,
                )
            )
    for what, copy in row_copies:
        if what < 2:
            copy.start()
    for copy in pack_copies:
        copy.start()
    for what, copy in row_copies:
        if what == 2:
            copy.start()

    def flux_of(t, plane, start, count=8):
        return flf[t, pl.ds(plane * PAD + start, count), :]

    def wrapped(value):
        return value - QUANTA * jnp.floor(value * (1.0 / QUANTA) + 0.5)

    def cell_phases(t, start, carry):
        if start < HALO:
            run = flux_of(t, 1, start + 1) - flux_of(t, 0, start + 1)
            for reach in (1, 2, 4):
                run = run + jnp.where(sub < 8 - reach, pltpu.roll(run, 8 - reach, 0), 0.0)
        else:
            run = flux_of(t, 0, start) - flux_of(t, 1, start)
            if start == HALO:
                run = jnp.where(sub == 0, 0.0, run)
            for reach in (1, 2, 4):
                run = run + jnp.where(sub >= reach, pltpu.roll(run, reach, 0), 0.0)
            if carry is not None:
                run = run + carry
        run = wrapped(run)
        chi[t, pl.ds(start, 8), :] = run
        th0, th3, th6 = (flux_of(t, plane, start) for plane in (0, 3, 6))
        rows = pl.ds(start, 8)
        span = pl.ds(t * LANES, LANES)
        px[A1, rows, span] = wrapped(run - th0 + QUANTA // 2)
        px[B2, rows, span] = wrapped(th6 + th3 + run + QUANTA // 2)
        px[B1, rows, span] = run
        px[A2, rows, span] = wrapped(th6 + run)
        return jnp.broadcast_to(run[7:8, :], (8, LANES))

    carries = []
    for t in range(2):
        carry = None
        for start in (HALO, HALO + 8):
            carry = cell_phases(t, start, carry)
            for orb in range(4):
                c, s = small_turn(px[orb, pl.ds(start, 8), pl.ds(t * LANES, LANES)], QUANTA)
                if orb in (A1, A2):
                    c, s = 0.5 * c, 0.5 * s
                gauge[orb, 0, t, pl.ds(start - HALO, 8), :] = c
                gauge[orb, 1, t, pl.ds(start - HALO, 8), :] = s
        carries.append(carry)

    def row_place(shape):
        at = lax.broadcasted_iota(jnp.int32, shape, 0)
        return jnp.where(at < COLS + HALO, at + HALO, jnp.where(at < COLS + SIDE, at - COLS - HALO, -1))

    def one_hot(here):
        return jnp.where(here, 1.0, 0.0).astype(jnp.bfloat16)

    at_row = row_place((TILES * LANES, LANES))
    at_lane = lax.rem(lax.broadcasted_iota(jnp.int32, (TILES * LANES, LANES), 1), SIDE) * DEEP

    def make_spread(y, carry):
        spread_m[:, pl.ds(pl.multiple_of(y * LANES, LANES), LANES)] = one_hot(at_row == at_lane + y)
        return carry

    lax.fori_loop(0, DEEP + 1, make_spread, 0)
    wide = lax.broadcasted_iota(jnp.int32, (COLS, TILES * LANES), 1)
    tall = lax.broadcasted_iota(jnp.int32, (COLS, TILES * LANES), 0)
    perm_m[...] = one_hot((tall + HALO == lax.rem(wide, SIDE) * DEEP + wide // SIDE) & (wide < SIDE * DEEP))
    wide = lax.broadcasted_iota(jnp.int32, (TILES * LANES, COLS), 1)
    tall = lax.broadcasted_iota(jnp.int32, (TILES * LANES, COLS), 0)
    back_m[...] = one_hot((wide + HALO == lax.rem(tall, SIDE) * DEEP + tall // SIDE) & (tall < SIDE * DEEP))

    def moved(value, matrix):
        parts = []
        for _ in range(3):
            parts.append(value.astype(jnp.bfloat16))
            value = value - parts[-1].astype(jnp.float32)
        out = jnp.dot(jnp.concatenate(parts, axis=0), matrix, preferred_element_type=jnp.float32)
        size = value.shape[0]
        return out[:size] + out[size : 2 * size] + out[2 * size :]

    lane_group = lane // SIDE

    def exchanged(values):
        values = list(values)
        for s in (1, 2, 4):
            keep = (lane_group // s) % 2 == 0
            for i in range(8):
                if not i & s:
                    one, two = values[i], values[i | s]
                    values[i] = jnp.where(keep, one, pltpu.roll(two, SIDE * s, 1))
                    values[i | s] = jnp.where(keep, pltpu.roll(one, LANES - SIDE * s, 1), two)
        return values

    def spread_angles(blocks):
        def spread_orbs(pair, carry):
            orbs = [2 * pair, 2 * pair + 1]
            places = [(orb, block) for orb in orbs for block in blocks]
            value = jnp.concatenate(
                [
                    jnp.concatenate(
                        [ang[t, :, orb, pl.ds(8 * block, 8), :].reshape(STATES * 8, LANES) for t in range(2)], axis=1
                    )
                    for orb, block in places
                ],
                axis=0,
            )
            out = moved(value, perm_m[...])
            for which, (orb, block) in enumerate(places):
                parts = [
                    [
                        out[64 * which + 8 * r : 64 * which + 8 * r + 8, LANES * t : LANES * t + LANES]
                        for r in range(8)
                    ]
                    for t in range(TILES)
                ]
                deep = exchanged(parts[0]) + exchanged(parts[1])
                last = parts[2][0]
                for r in range(1, 8):
                    last = jnp.where(lane_group == r, pltpu.roll(parts[2][r], SIDE * r, 1), last)
                for y, value in enumerate(deep + [last]):
                    af[orb, y, pl.ds(8 * block, 8), :] = value
            return carry

        lax.fori_loop(0, 2, spread_orbs, 0)

    spread_angles((1, 2))

    for what, copy in row_copies:
        if what < 2:
            copy.wait()
    for t in range(2):
        for start in (0, HALO + ROWS):
            flux_to_float(t, start, HALO)
            cell_phases(t, start, carries[t])
    for copy in pack_copies:
        copy.wait()

    beside = lax.rem(lane, SIDE)

    def unpack(what, block):
        return jnp.where(beside < HALO, got[1, block, what], got[0, block, what])

    for block in range(BLOCKS):
        values = unpack(4, block)
        for which in range(8):
            move = (LANES - SIDE * which) % LANES
            flf[2, pl.ds(which * PAD + 8 * block, 8), :] = pltpu.roll(values, move, 1) if move else values
    carry = None
    for start in (HALO, HALO + 8, HALO + ROWS, 0):
        carry = cell_phases(2, start, carry)

    def right(values):
        rolled = [pltpu.roll(value, 1, 1) for value in values]
        edges = [pltpu.roll(values[2], LANES - SIDE + 1, 1), rolled[0], rolled[1]]
        return [jnp.where(first_lane, edges[t], rolled[t]) for t in range(TILES)]

    def left(values):
        rolled = [pltpu.roll(value, LANES - 1, 1) for value in values]
        edge = pltpu.roll(values[0], SIDE - 1, 1)
        return [
            jnp.where(last_lane, rolled[1], rolled[0]),
            jnp.where(last_lane, rolled[2], rolled[1]),
            jnp.where(lane == SIDE - 1, edge, rolled[2]),
        ]

    for start in range(0, EXT, 8):
        rows = pl.ds(start, 8)
        th = [[flux_of(t, plane, start) for plane in range(8)] for t in range(TILES)]
        cell = [chi[t, rows, :] for t in range(TILES)]
        cell_left, cell_right = right(cell), left(cell)
        far = left([th[t][6] + th[t][3] for t in range(TILES)])
        for t in range(TILES):
            span = pl.ds(t * LANES, LANES)
            below = [flux_of(t, plane, start + 1) for plane in (6, 3, 1, 0)]
            px[4, rows, span] = wrapped(th[t][2] - th[t][0] + cell[t] - cell_left[t])
            px[5, rows, span] = wrapped(th[t][4] + th[t][6] - below[0] - below[1] + below[2] - below[3])
            px[6, rows, span] = wrapped(th[t][5] + th[t][6] - far[t] + cell[t] - cell_right[t])
            rest = th[t][7]
            for part in range(3):
                head = rest.astype(jnp.bfloat16).astype(jnp.float32)
                px[7 + part, rows, span] = head
                rest = rest - head

    planes = px[...].reshape(10 * EXT, TILES * LANES).astype(jnp.bfloat16)
    lane_place = lax.rem(lane, SIDE) * DEEP
    sub_i = gx * ROWS - HALO + sub

    def cell_inside(y, block):
        j = gy * COLS - HALO + lane_place + y
        i = sub_i + 8 * block
        return (j >= 0) & (j < ny) & (i >= 0) & (i < nx)

    def make_tables(pair, carry):
        two = jnp.dot(
            planes,
            spread_m[:, pl.ds(pl.multiple_of(pair * (2 * LANES), 2 * LANES), 2 * LANES)],
            preferred_element_type=jnp.float32,
        )
        for one in range(2):
            y = 2 * pair + one
            out = two[:, LANES * one : LANES * one + LANES]
            place = lane_place + y
            j = gy * COLS - HALO + place
            for block in range(BLOCKS):
                rows = pl.ds(ROW0 + 8 * block, 8)
                part = [out[which * EXT + 8 * block : which * EXT + 8 * block + 8, :] for which in range(10)]
                for orb in range(4):
                    phf[orb, y, pl.ds(8 * block, 8), :] = part[orb] * (1.0 / QUANTA)
                here = cell_inside(y, block)
                for which, good in (
                    (T2C, here & (j >= 1) & (place >= 1)),
                    (T4C, here & (sub_i + 8 * block + 1 < nx)),
                    (T5C, here & (j + 1 < ny) & (place < SIDE * DEEP - 1)),
                ):
                    c, s = small_turn(part[4 + which // 2], QUANTA)
                    ft[which, y + 1, rows, :] = jnp.where(good, c, 0.0)
                    ft[which + 1, y + 1, rows, :] = jnp.where(good, s, 0.0)
                ft[CPL, y + 1, rows, :] = jnp.where(here, part[7] + part[8] + part[9], 0.0)
        return carry

    lax.fori_loop(0, (DEEP + 1) // 2, make_tables, 0)
    for block in range(BLOCKS):
        rows = pl.ds(ROW0 + 8 * block, 8)
        for which in (T2C, T2S):
            ft[which, DEEP + 1, rows, :] = pltpu.roll(ft[which, 1, rows, :], LANES - 1, 1)
        for which in (T5C, T5S):
            ft[which, 0, rows, :] = pltpu.roll(ft[which, DEEP, rows, :], 1, 1)

    def start_values(blocks):
        def start_one(pair, carry):
            for y in (2 * pair, 2 * pair + 1):
                place = lane_place + y
                beyond = (place < HALO) | (place >= COLS + HALO)
                move = jnp.where(y <= HALO, LANES - HALO - y, SIDE + HALO - y)
                for block in blocks:
                    here = cell_inside(y, block)
                    rows = pl.ds(8 * block, 8)
                    for orb in range(4):
                        angle = jnp.where(beyond, pltpu.roll(unpack(orb, block), move, 1), af[orb, y, rows, :])
                        c, s = turn(
                            angle * (0.5 / math.pi) + phf[orb, y, rows, :], 2.0 if orb in (A1, A2) else 1.0
                        )
                        u[0, 2 * orb, y + 1, pl.ds(ROW0 + 8 * block, 8), :] = jnp.where(here, c, 0.0)
                        u[0, 2 * orb + 1, y + 1, pl.ds(ROW0 + 8 * block, 8), :] = jnp.where(here, s, 0.0)
            return carry

        lax.fori_loop(0, (DEEP + 1) // 2, start_one, 0)

    start_values((1, 2))
    for what, copy in row_copies:
        if what == 2:
            copy.wait()
    spread_angles((0, 3))
    start_values((0, 3))

    def site(buf, orb, y, row):
        rows = pl.ds(ROW0 + row, 8)
        return u[buf, 2 * orb, y + 1, rows, :], u[buf, 2 * orb + 1, y + 1, rows, :]

    def table(which, y, row):
        rows = pl.ds(ROW0 + row, 8)
        return ft[which, y + 1, rows, :], ft[which + 1, y + 1, rows, :]

    def join(buf, row):
        rows = pl.ds(ROW0 + row, 8)
        for part in range(2):
            for orb in (B1, A2):
                u[buf, 2 * orb + part, 0, rows, :] = pltpu.roll(u[buf, 2 * orb + part, DEEP, rows, :], 1, 1)
            for orb in (A1, B2):
                u[buf, 2 * orb + part, DEEP + 1, rows, :] = pltpu.roll(u[buf, 2 * orb + part, 1, rows, :], LANES - 1, 1)

    for block in range(BLOCKS):
        join(0, 8 * block)

    def velocity(y, carry):
        place = lane_place + y
        own = jnp.where((place >= HALO) & (place < COLS + HALO), 0.5, 0.0)
        for block in range(2):
            row = HALO + 8 * block
            v = [None] * 4
            v[A1] = [own * part for part in site(0, B1, y, row - 1)]
            v[B1] = [-own * part for part in site(0, A1, y, row + 1)]
            v[A2] = [-own * part for part in rot(*table(T4C, y, row), site(0, B2, y, row + 1))]
            v[B2] = [own * part for part in rot_back(*table(T4C, y, row - 1), site(0, A2, y, row - 1))]
            for orb in range(4):
                for part in range(2):
                    vel[y, block, 2 * orb + part] = v[orb][part]
        return carry

    lax.fori_loop(0, DEEP, velocity, 0)

    def step_at(src, dst, y, row, first):
        a1, b2, b1, a2 = (site(src, orb, y, row) for orb in range(4))
        hop = ft[CPL, y + 1, pl.ds(ROW0 + row, 8), :]
        new = [None] * 4
        new[A1] = add(b1, site(src, B1, y, row - 1), rot(*table(T2C, y, row), site(src, B1, y - 1, row)))
        new[B1] = add(
            a1,
            site(src, A1, y, row + 1),
            rot_back(*table(T2C, y + 1, row), site(src, A1, y + 1, row)),
            (hop * a2[0], hop * a2[1]),
        )
        new[A2] = add(
            b2,
            rot(*table(T4C, y, row), site(src, B2, y, row + 1)),
            rot(*table(T5C, y, row), site(src, B2, y + 1, row)),
            (hop * b1[0], hop * b1[1]),
        )
        new[B2] = add(
            a2,
            rot_back(*table(T4C, y, row - 1), site(src, A2, y, row - 1)),
            rot_back(*table(T5C, y - 1, row), site(src, A2, y - 1, row)),
        )
        for orb in range(4):
            size = 1.0 if orb in (A1, A2) else 0.25
            for part in range(2):
                value = new[orb][part]
                rows = pl.ds(ROW0 + row, 8)
                if first:
                    value = (0.5 * size) * value
                else:
                    value = (value if size == 1.0 else size * value) - u[dst, 2 * orb + part, y + 1, rows, :]
                u[dst, 2 * orb + part, y + 1, rows, :] = value

    def step(src, dst, rows, first=False):
        def step_two(pair, carry):
            for row in rows:
                step_at(src, dst, 2 * pair, row, first)
                step_at(src, dst, 2 * pair + 1, row, first)
            return carry

        for row in rows:
            step_at(src, dst, DEEP - 1, row, first)
        lax.fori_loop(0, DEEP // 2, step_two, 0)
        for row in rows:
            join(dst, row)

        @pl.when(gx == 0)
        def _():
            for orb in (B1, A2):
                for part in range(2):
                    u[dst, 2 * orb + part, :, pl.ds(ROW0 + HALO - 1, 1), :] = jnp.zeros((DEEP + 2, 1, LANES), jnp.float32)

        @pl.when(gx == gx_size - 1)
        def _():
            for orb in (A1, B2):
                for part in range(2):
                    u[dst, 2 * orb + part, :, pl.ds(ROW0 + HALO + ROWS, 1), :] = jnp.zeros((DEEP + 2, 1, LANES), jnp.float32)

    def gather(k):
        def gather_at(y, sums):
            sums = list(sums)
            for block in range(2):
                for orb in range(4):
                    vr, vi = vel[y, block, 2 * orb], vel[y, block, 2 * orb + 1]
                    for which in range(2):
                        ur, ui = site(which, orb, y, HALO + 8 * block)
                        hist[k + which, y, block, 2 * orb], hist[k + which, y, block, 2 * orb + 1] = ur, ui
                        sums[2 * which] += vr * ur + vi * ui
                        sums[2 * which + 1] += vr * ui - vi * ur
            return tuple(sums)

        def gather_two(pair, sums):
            return gather_at(2 * pair + 1, gather_at(2 * pair, sums))

        sums = gather_at(DEEP - 1, lax.fori_loop(0, DEEP // 2, gather_two, (zero,) * 4))
        for which in range(4):
            mom[2 * k + which] = sums[which]

    far_rows, mid_rows, own_rows = (0, 8, 16, 24), (4, 12, 20), (8, 16)
    step(0, 1, far_rows, first=True)
    gather(0)

    def early(m, carry):
        step(1, 0, far_rows)
        step(0, 1, far_rows)
        gather(2 * m)
        return carry

    def late(m, carry):
        step(1, 0, mid_rows)
        step(0, 1, mid_rows)
        gather(2 * m)
        return carry

    lax.fori_loop(1, 4, early, 0)
    lax.fori_loop(4, TERMS // 2 - 1, late, 0)
    step(1, 0, mid_rows)
    step(0, 1, own_rows)
    gather(TERMS - 2)

    sums = []
    for part in (1, 0):
        for k in range(TERMS):
            sums.append(jnp.sum(mom[2 * k + part], axis=0, keepdims=True))
    state = lax.broadcasted_iota(jnp.int32, (STATES, LANES), 0)
    ones = jnp.where(lane_group == state, 1.0, 0.0)
    local = lax.dot_general(
        ones,
        jnp.concatenate(sums + [jnp.zeros((LANES - 2 * TERMS, LANES), jnp.float32)], axis=0),
        (((1,), (1,)), ((), ())),
        precision=lax.Precision.HIGHEST,
        preferred_element_type=jnp.float32,
    )
    local = jnp.where(lane < TERMS, local, -local) * (1.0 / math.sqrt(4.0 * nx * ny))
    wide = 2 * TERMS
    spread_out = zero
    for q in range(4):
        value = pltpu.roll(local, wide * q, 1) if q else local
        spread_out = jnp.where((lax.rem(sub, 4) == q) & (lane // wide == q), value, spread_out)
    folded = jnp.concatenate(
        [jnp.sum(spread_out[:4], axis=0, keepdims=True), jnp.sum(spread_out[4:], axis=0, keepdims=True)], axis=0
    )

    def spread(value, msg, slots, me, size, peer, send_sem, recv_sem):
        msg[...] = value
        slots[me] = value

        def copy_to(other, slot, d):
            return pltpu.make_async_remote_copy(
                src_ref=msg,
                dst_ref=slots.at[slot],
                send_sem=send_sem.at[d],
                recv_sem=recv_sem.at[slot],
                device_id=peer(other),
                device_id_type=MESH,
            )

        def send(d, carry):
            copy_to(lax.rem(me + d, size), me, d).start()
            return carry

        def finish(d, carry):
            other = lax.rem(me + d, size)
            copy_to(other, me, d).wait_send()
            copy_to(other, other, d).wait_recv()
            return carry

        lax.fori_loop(1, size, send, 0)
        return lambda: lax.fori_loop(1, size, finish, 0)

    def total(slots, size):
        value = slots[0]
        for at in range(1, size):
            value = value + slots[at]
        return value

    def out_copy(orb):
        return pltpu.make_async_copy(outv.at[:, :, orb], evo_h.at[:, :, orb], out_sem.at[orb])

    def evolve(orb, carry):
        def evolve_one(y, carry):
            for block in range(2):
                re, im = zero, zero
                for m in range(TERMS // 2):
                    a, b = ((hist[2 * m + n, y, block, 2 * orb], hist[2 * m + n, y, block, 2 * orb + 1]) for n in range(2))
                    re = re + (EVEN[m] * a[0] - ODD[m] * b[1])
                    im = im + (EVEN[m] * a[1] + ODD[m] * b[0])
                tf[block, y], tf[2 + block, y] = re, im
            return carry

        lax.fori_loop(0, DEEP, evolve_one, 0)

        def back(which, carry):
            tiles = [exchanged([tf[which, 8 * t + i] for i in range(8)]) for t in range(2)]
            last = tf[which, DEEP - 1]
            tiles.append([pltpu.roll(last, LANES - SIDE * r, 1) if r else last for r in range(8)])
            for t in range(TILES):
                for r in range(8):
                    tl[which, pl.ds(8 * r, 8), pl.ds(LANES * t, LANES)] = tiles[t][r]
            return carry

        lax.fori_loop(0, 4, back, 0)
        out = moved(tl[...].reshape(4 * 64, TILES * LANES), back_m[...])
        for block in range(2):
            rows = pl.ds(8 * block, 8)
            c = jnp.concatenate([gauge[orb, 0, t, rows, :] for t in range(2)], axis=1)
            s = jnp.concatenate([gauge[orb, 1, t, rows, :] for t in range(2)], axis=1)
            for r in range(8):
                at = 64 * block + 8 * r
                v = rot_back(c, s, (out[at : at + 8, :], out[128 + at : 128 + at + 8, :]))
                outv[0, r, orb, rows, :], outv[1, r, orb, rows, :] = v
        out_copy(orb).start()
        return carry

    finish_1 = spread(folded, msg_1, in_1, place_1, group_1, peer_1, s1_sem, r1_sem)
    lax.fori_loop(0, 2, evolve, 0)
    finish_1()
    finish_2 = spread(total(in_1, group_1), msg_2, in_2, place_2, group_2, peer_2, s2_sem, r2_sem)
    lax.fori_loop(2, 4, evolve, 0)
    finish_2()
    folded = total(in_2, group_2)
    rows = jnp.where(sub < 4, folded[0:1, :], folded[1:2, :])
    result = rows
    for q in range(1, 4):
        result = jnp.where(lax.rem(sub, 4) == q, pltpu.roll(rows, LANES - wide * q, 1), result)
    mom_ref[0] = result[:, :TERMS]
    mom_ref[1] = pltpu.roll(result, LANES - TERMS, 1)[:, :TERMS]
    for orb in range(4):
        out_copy(orb).wait()


def per_device(nx, ny, gx_size, gy_size, angles, bond_flux, coupling):
    f32 = jnp.float32
    tile = (STATES, LANES)
    group_1, group_2 = gx_size // 2, 2 * gy_size
    evolved, moments = pl.pallas_call(
        functools.partial(kernel, nx, ny, gx_size, gy_size),
        out_shape=(
            jax.ShapeDtypeStruct((2, STATES, 4, ROWS, COLS), f32),
            jax.ShapeDtypeStruct((2, STATES, TERMS), f32),
        ),
        in_specs=[pl.BlockSpec(memory_space=pl.ANY)] * 3,
        out_specs=(pl.BlockSpec(memory_space=pl.ANY), pl.BlockSpec(memory_space=pltpu.VMEM)),
        scratch_shapes=[
            pltpu.VMEM((2, STATES, 4, EXT, LANES), f32),
            pltpu.VMEM((2, 7, EXT, LANES), jnp.int32),
            pltpu.VMEM((TILES, 8 * PAD, LANES), f32),
            pltpu.VMEM((2, 8, DEEP + 2, EXT + 2 * ROW0, LANES), f32),
            pltpu.VMEM((TERMS, DEEP, 2, 8) + tile, f32),
            pltpu.VMEM((7, DEEP + 2, EXT + 2 * ROW0, LANES), f32),
            pltpu.VMEM((4, DEEP + 1, EXT, LANES), f32),
            pltpu.VMEM((4, DEEP + 1, EXT, LANES), f32),
            pltpu.VMEM((10, EXT, TILES * LANES), f32),
            pltpu.VMEM((TILES * LANES, (DEEP + 1) * LANES), jnp.bfloat16),
            pltpu.VMEM((COLS, TILES * LANES), jnp.bfloat16),
            pltpu.VMEM((TILES * LANES, COLS), jnp.bfloat16),
            pltpu.VMEM((4, 2, 2, ROWS, LANES), f32),
            pltpu.VMEM((TILES, EXT, LANES), f32),
            pltpu.VMEM((DEEP, 2, 8) + tile, f32),
            pltpu.VMEM((4, DEEP) + tile, f32),
            pltpu.VMEM((4, 64, TILES * LANES), f32),
            pltpu.VMEM((2, STATES, 4, ROWS, COLS), f32),
            pltpu.VMEM((2 * TERMS,) + tile, f32),
            pltpu.VMEM((2, 2, 5) + tile, f32),
            pltpu.VMEM((2, BLOCKS, 5) + tile, f32),
            pltpu.VMEM((2, LANES), f32),
            pltpu.VMEM((2, LANES), f32),
            pltpu.VMEM((group_1, 2, LANES), f32),
            pltpu.VMEM((group_2, 2, LANES), f32),
            pltpu.SemaphoreType.DMA((2, 3)),
            pltpu.SemaphoreType.DMA((4,)),
            pltpu.SemaphoreType.DMA((2, 2, 3)),
            pltpu.SemaphoreType.DMA((2, 2, 3)),
            pltpu.SemaphoreType.DMA((2, 3)),
            pltpu.SemaphoreType.DMA((2, 3)),
            pltpu.SemaphoreType.DMA((group_1,)),
            pltpu.SemaphoreType.DMA((group_1,)),
            pltpu.SemaphoreType.DMA((group_2,)),
            pltpu.SemaphoreType.DMA((group_2,)),
        ],
        compiler_params=pltpu.CompilerParams(
            collective_id=0, has_side_effects=True, vmem_limit_bytes=60 * 2**20
        ),
        name="evolve",
    )(angles, bond_flux, coupling)
    return evolved, jnp.transpose(moments, (2, 0, 1))


def solution(mesh):
    in_specs = (P(None, None, "gx", "gy"), P(None, "gx", "gy"), P("gx", "gy"))
    out_specs = (P(None, None, None, "gx", "gy"), P())
    gx_size, gy_size = mesh.shape["gx"], mesh.shape["gy"]
    return jax.shard_map(
        functools.partial(per_device, gx_size * ROWS, gy_size * COLS, gx_size, gy_size),
        mesh=mesh,
        in_specs=in_specs,
        out_specs=out_specs,
        check_vma=False,
    )
```

```python
import functools
import math

import jax
import jax.numpy as jnp
import numpy as np
from jax import lax
from jax.experimental import pallas as pl
from jax.experimental.pallas import tpu as pltpu
from jax.sharding import PartitionSpec as P

TERMS = 16
QUANTA = 64
PHASE_SPAN = 12.0

STATES = 8
ROWS = 16
COLS = 256
LANES = 128
HALO = 8
EXT = ROWS + 2 * HALO
PAD = EXT + 8
BLOCKS = EXT // 8
SIDE = 2 * HALO
TILES = 3
DEEP = (COLS + SIDE) // 16
ROW0 = 8
UNROLL = 1
A1, B2, B1, A2 = 0, 1, 2, 3
MESH = pl.DeviceIdType.MESH

T2C, T2S, T4C, T4S, T5C, T5S, CPL = range(7)


def bessel_value(degree, argument):
    running = 0.0
    for number in range(60):
        running += (
            (-1.0) ** number
            * (argument / 2.0) ** (2 * number + degree)
            / (math.factorial(number) * math.factorial(number + degree))
        )
    return running


EVEN = [(1.0 if m == 0 else 2.0) * (-1.0) ** m * bessel_value(2 * m, PHASE_SPAN) for m in range(TERMS // 2)]
ODD = [-2.0 * (-1.0) ** m * bessel_value(2 * m + 1, PHASE_SPAN) for m in range(TERMS // 2)]

def fitted(function, terms):
    nodes = 0.125 - 0.125 * np.cos(math.pi * (np.arange(40) + 0.5) / 40)
    fit = np.polynomial.chebyshev.Chebyshev.fit(nodes, function(np.sqrt(nodes)), terms - 1, domain=[0.0, 0.25])
    return [float(value) for value in fit.convert(kind=np.polynomial.Polynomial).coef]


SIN_COEF = fitted(lambda r: np.sin(math.pi * r) / r, 5)
COS_COEF = fitted(lambda r: np.cos(math.pi * r), 6)


def small_turn(p, unit=1, size=1.0):
    q = p * p
    s, c = SIN_COEF[-1] / unit ** (2 * len(SIN_COEF) - 1), COS_COEF[-1] / unit ** (2 * len(COS_COEF) - 2)
    for power in reversed(range(len(SIN_COEF) - 1)):
        s = s * q + SIN_COEF[power] / unit ** (2 * power + 1)
    for power in reversed(range(len(COS_COEF) - 1)):
        c = c * q + COS_COEF[power] / unit ** (2 * power)
    s = s * p
    twice = (2.0 * size) * s
    return size - twice * s, twice * c


def turn(f, size=1.0):
    return small_turn(f - jnp.floor(f + 0.5), 1, size)


def rot(c, s, v):
    return c * v[0] - s * v[1], s * v[0] + c * v[1]


def rot_back(c, s, v):
    return c * v[0] + s * v[1], c * v[1] - s * v[0]


def add(*pairs):
    re, im = pairs[0]
    for pair in pairs[1:]:
        re, im = re + pair[0], im + pair[1]
    return re, im


def kernel(
    nx, ny, gx_size, gy_size,
    ang_h, flux_h, coup_h, evo_h, mom_ref,
    ang, fli, flf, u, hist, ft, phf, af, px, spread_m, perm_m, back_m, gauge, chi, vel, tf, tl, outv, mom, pack, msg_own, msg_far, got_own, got_far, halo, msg_1, msg_2, in_1, in_2,
    load_sem, out_sem, xs_sem, xr_sem, ps_sem, pr_sem, s1_sem, r1_sem, s2_sem, r2_sem,
):
    gx, gy = lax.axis_index("gx"), lax.axis_index("gy")
    group_1, group_2 = gx_size // 2, 2 * gy_size
    half, place_1 = gx // group_1, lax.rem(gx, group_1)
    place_2 = half * gy_size + gy

    def near(dx, dy):
        return (lax.rem(gx + dx + gx_size, gx_size), lax.rem(gy + dy + gy_size, gy_size))

    def peer_1(other):
        return (half * group_1 + other, gy)

    def peer_2(other):
        return (other // gy_size * group_1 + place_1, lax.rem(other, gy_size))

    lane = lax.broadcasted_iota(jnp.int32, (STATES, LANES), 1)
    sub = lax.broadcasted_iota(jnp.int32, (8, LANES), 0)
    first_lane, last_lane = lane == 0, lane == LANES - 1
    zero = jnp.zeros((STATES, LANES), jnp.float32)

    loads = []
    for t in range(2):
        span = pl.ds(t * LANES, LANES)
        own = pl.ds(HALO, ROWS)
        loads.append(pltpu.make_async_copy(flux_h.at[:, :, span], fli.at[t, :, own, :], load_sem.at[t, 0]))
        loads.append(pltpu.make_async_copy(coup_h.at[:, span], flf.at[t, pl.ds(7 * PAD + HALO, ROWS), :], load_sem.at[t, 1]))
        loads.append(pltpu.make_async_copy(ang_h.at[:, :, :, span], ang.at[t, :, :, own, :], load_sem.at[t, 2]))
    for copy in loads:
        copy.start()

    barrier = pltpu.get_barrier_semaphore()

    def greet(peer, me, size):
        def one(d, carry):
            pl.semaphore_signal(barrier, inc=1, device_id=peer(lax.rem(me + d, size)), device_id_type=MESH)
            return carry

        lax.fori_loop(1, size, one, 0)

    for dx in (-1, 0, 1):
        for dy in (-1, 0, 1):
            if dx or dy:
                pl.semaphore_signal(barrier, inc=1, device_id=near(dx, dy), device_id_type=MESH)
    greet(peer_1, place_1, group_1)
    greet(peer_2, place_2, group_2)

    for t in range(TILES):
        for plane in range(8):
            flf[t, pl.ds(plane * PAD + EXT, 8), :] = zero

    for copy in loads:
        copy.wait()

    def flux_to_float(t, start, count):
        for plane in range(7):
            flf[t, pl.ds(plane * PAD + start, count), :] = fli[t, plane, pl.ds(start, count), :].astype(jnp.float32)

    for t in range(2):
        flux_to_float(t, HALO, ROWS)

    group = lane // HALO

    def packed(side, value_of):
        out = zero
        for r in range(8):
            value = value_of(r)
            move = (SIDE * r + (SIDE if side == 0 else 0)) % LANES
            if move:
                value = pltpu.roll(value, move, 1)
            out = jnp.where(group == 2 * r + 1 - side, value, out)
        return out

    def pack_angles(orb, carry):
        for side in range(2):
            for block in range(2):
                rows = pl.ds(HALO + 8 * block, 8)
                pack[side, block, orb] = packed(side, lambda r: ang[1 - side, r, orb, rows, :])
        return carry

    lax.fori_loop(0, 4, pack_angles, 0)
    for side in range(2):
        for block in range(2):
            pack[side, block, 4] = packed(side, lambda r: flf[1 - side, pl.ds(r * PAD + HALO + 8 * block, 8), :])

    def pushed(value, side):
        return pltpu.roll(value, LANES - HALO if side == 0 else HALO, 1)

    for side in range(2):
        for what in range(5):
            msg_own[side, what] = pack[side, 0, what] + pushed(pack[side, 1, what], side)
        for block in range(2):
            for what in range(2):
                msg_far[side, block, what] = pack[side, block, 2 * what] + pushed(pack[side, block, 2 * what + 1], side)
            msg_far[side, block, 2] = pack[side, block, 4]

    def flux_of(t, plane, start, count=8):
        return flf[t, pl.ds(plane * PAD + start, count), :]

    def wrapped(value):
        return value - QUANTA * jnp.floor(value * (1.0 / QUANTA) + 0.5)

    def cell_phases(t, start, carry):
        if start < HALO:
            run = flux_of(t, 1, start + 1) - flux_of(t, 0, start + 1)
            for reach in (1, 2, 4):
                run = run + jnp.where(sub < 8 - reach, pltpu.roll(run, 8 - reach, 0), 0.0)
        else:
            run = flux_of(t, 0, start) - flux_of(t, 1, start)
            if start == HALO:
                run = jnp.where(sub == 0, 0.0, run)
            for reach in (1, 2, 4):
                run = run + jnp.where(sub >= reach, pltpu.roll(run, reach, 0), 0.0)
            if carry is not None:
                run = run + carry
        run = wrapped(run)
        chi[t, pl.ds(start, 8), :] = run
        th0, th3, th6 = (flux_of(t, plane, start) for plane in (0, 3, 6))
        rows = pl.ds(start, 8)
        span = pl.ds(t * LANES, LANES)
        px[A1, rows, span] = wrapped(run - th0 + QUANTA // 2)
        px[B2, rows, span] = wrapped(th6 + th3 + run + QUANTA // 2)
        px[B1, rows, span] = run
        px[A2, rows, span] = wrapped(th6 + run)
        return jnp.broadcast_to(run[7:8, :], (8, LANES))

    carries = []
    for t in range(2):
        carry = None
        for start in (HALO, HALO + 8):
            carry = cell_phases(t, start, carry)
            for orb in range(4):
                c, s = small_turn(px[orb, pl.ds(start, 8), pl.ds(t * LANES, LANES)], QUANTA)
                if orb in (A1, A2):
                    c, s = 0.5 * c, 0.5 * s
                gauge[orb, 0, t, pl.ds(start - HALO, 8), :] = c
                gauge[orb, 1, t, pl.ds(start - HALO, 8), :] = s
        carries.append(carry)

    def row_place(shape):
        at = lax.broadcasted_iota(jnp.int32, shape, 0)
        return jnp.where(at < COLS + HALO, at + HALO, jnp.where(at < COLS + SIDE, at - COLS - HALO, -1))

    def one_hot(here):
        return jnp.where(here, 1.0, 0.0).astype(jnp.bfloat16)

    at_row = row_place((TILES * LANES, LANES))
    at_lane = lax.rem(lax.broadcasted_iota(jnp.int32, (TILES * LANES, LANES), 1), SIDE) * DEEP

    def make_spread(y, carry):
        spread_m[:, pl.ds(pl.multiple_of(y * LANES, LANES), LANES)] = one_hot(at_row == at_lane + y)
        return carry

    lax.fori_loop(0, DEEP + 1, make_spread, 0)
    wide = lax.broadcasted_iota(jnp.int32, (COLS, TILES * LANES), 1)
    tall = lax.broadcasted_iota(jnp.int32, (COLS, TILES * LANES), 0)
    perm_m[...] = one_hot((tall + HALO == lax.rem(wide, SIDE) * DEEP + wide // SIDE) & (wide < SIDE * DEEP))
    wide = lax.broadcasted_iota(jnp.int32, (TILES * LANES, COLS), 1)
    tall = lax.broadcasted_iota(jnp.int32, (TILES * LANES, COLS), 0)
    back_m[...] = one_hot((wide + HALO == lax.rem(tall, SIDE) * DEEP + tall // SIDE) & (tall < SIDE * DEEP))

    def moved(value, matrix):
        parts = []
        for _ in range(3):
            parts.append(value.astype(jnp.bfloat16))
            value = value - parts[-1].astype(jnp.float32)
        out = jnp.dot(jnp.concatenate(parts, axis=0), matrix, preferred_element_type=jnp.float32)
        size = value.shape[0]
        return out[:size] + out[size : 2 * size] + out[2 * size :]

    lane_group = lane // SIDE

    def exchanged(values):
        values = list(values)
        for s in (1, 2, 4):
            keep = (lane_group // s) % 2 == 0
            for i in range(8):
                if not i & s:
                    one, two = values[i], values[i | s]
                    values[i] = jnp.where(keep, one, pltpu.roll(two, SIDE * s, 1))
                    values[i | s] = jnp.where(keep, pltpu.roll(one, LANES - SIDE * s, 1), two)
        return values

    def spread_angles(blocks):
        def spread_orbs(pair, carry):
            orbs = [2 * pair, 2 * pair + 1]
            places = [(orb, block) for orb in orbs for block in blocks]
            value = jnp.concatenate(
                [
                    jnp.concatenate(
                        [ang[t, :, orb, pl.ds(8 * block, 8), :].reshape(STATES * 8, LANES) for t in range(2)], axis=1
                    )
                    for orb, block in places
                ],
                axis=0,
            )
            out = moved(value, perm_m[...])
            for which, (orb, block) in enumerate(places):
                parts = [
                    [
                        out[64 * which + 8 * r : 64 * which + 8 * r + 8, LANES * t : LANES * t + LANES]
                        for r in range(8)
                    ]
                    for t in range(TILES)
                ]
                deep = exchanged(parts[0]) + exchanged(parts[1])
                last = parts[2][0]
                for r in range(1, 8):
                    last = jnp.where(lane_group == r, pltpu.roll(parts[2][r], SIDE * r, 1), last)
                for y, value in enumerate(deep + [last]):
                    af[orb, y, pl.ds(8 * block, 8), :] = value
            return carry

        lax.fori_loop(0, 2, spread_orbs, 0)

    spread_angles((1, 2))

    pl.semaphore_wait(barrier, 8 + group_1 - 1 + group_2 - 1)

    row_copies = []
    for side, dx in ((0, 1), (1, -1)):
        src_rows = pl.ds(ROWS - HALO, HALO) if side == 0 else pl.ds(0, HALO)
        low = 0 if side == 0 else HALO + ROWS
        for t in range(2):
            span = pl.ds(t * LANES, LANES)
            for what, (src, dst) in enumerate(
                (
                    (flux_h.at[:, src_rows, span], fli.at[t, :, pl.ds(low, HALO), :]),
                    (coup_h.at[src_rows, span], flf.at[t, pl.ds(7 * PAD + low, HALO), :]),
                    (ang_h.at[:, :, src_rows, span], ang.at[t, :, :, pl.ds(low, HALO), :]),
                )
            ):
                row_copies.append(
                    (
                        what,
                        pltpu.make_async_remote_copy(
                            src_ref=src,
                            dst_ref=dst,
                            send_sem=xs_sem.at[side, t, what],
                            recv_sem=xr_sem.at[side, t, what],
                            device_id=near(dx, 0),
                            device_id_type=MESH,
                        ),
                    )
                )
    pack_copies = []
    for side, dy in ((0, 1), (1, -1)):
        for dx, src, dst, cut in (
            (0, msg_own.at[side], got_own.at[side], 4),
            (1, msg_far.at[side, 1], got_far.at[side, 0], 2),
            (-1, msg_far.at[side, 0], got_far.at[side, 1], 2),
        ):
            for late, part in enumerate((pl.ds(cut, 1), pl.ds(0, cut))):
                pack_copies.append(
                    (
                        late,
                        pltpu.make_async_remote_copy(
                            src_ref=src.at[part],
                            dst_ref=dst.at[part],
                            send_sem=ps_sem.at[side, 1 - dx, late],
                            recv_sem=pr_sem.at[side, 1 - dx, late],
                            device_id=near(dx, dy),
                            device_id_type=MESH,
                        ),
                    )
                )
    for late, copy in pack_copies:
        if not late:
            copy.start()
    for what, copy in row_copies:
        if what < 2:
            copy.start()
    for late, copy in pack_copies:
        if late:
            copy.start()
    for what, copy in row_copies:
        if what == 2:
            copy.start()


    for what, copy in row_copies:
        if what < 2:
            copy.wait()
    for t in range(2):
        for start in (0, HALO + ROWS):
            flux_to_float(t, start, HALO)
            cell_phases(t, start, carries[t])
    for late, copy in pack_copies:
        if not late:
            copy.wait()

    beside = lax.rem(lane, SIDE)

    def pulled(value, side):
        return pltpu.roll(value, HALO if side == 0 else LANES - HALO, 1)

    def merge(what, block):
        sides = []
        for side in range(2):
            if block in (1, 2):
                value = got_own[side, what]
                sides.append(pulled(value, side) if block == 2 else value)
            else:
                value = got_far[side, 0 if block == 0 else 1, 2 if what == 4 else what // 2]
                sides.append(pulled(value, side) if what in (1, 3) else value)
        return jnp.where(beside < HALO, sides[1], sides[0])

    for block in range(BLOCKS):
        values = merge(4, block)
        for which in range(8):
            move = (LANES - SIDE * which) % LANES
            flf[2, pl.ds(which * PAD + 8 * block, 8), :] = pltpu.roll(values, move, 1) if move else values
    carry = None
    for start in (HALO, HALO + 8, HALO + ROWS, 0):
        carry = cell_phases(2, start, carry)

    def right(values):
        rolled = [pltpu.roll(value, 1, 1) for value in values]
        edges = [pltpu.roll(values[2], LANES - SIDE + 1, 1), rolled[0], rolled[1]]
        return [jnp.where(first_lane, edges[t], rolled[t]) for t in range(TILES)]

    def left(values):
        rolled = [pltpu.roll(value, LANES - 1, 1) for value in values]
        edge = pltpu.roll(values[0], SIDE - 1, 1)
        return [
            jnp.where(last_lane, rolled[1], rolled[0]),
            jnp.where(last_lane, rolled[2], rolled[1]),
            jnp.where(lane == SIDE - 1, edge, rolled[2]),
        ]

    for start in range(0, EXT, 8):
        rows = pl.ds(start, 8)
        th = [[flux_of(t, plane, start) for plane in range(8)] for t in range(TILES)]
        cell = [chi[t, rows, :] for t in range(TILES)]
        cell_left, cell_right = right(cell), left(cell)
        far = left([th[t][6] + th[t][3] for t in range(TILES)])
        for t in range(TILES):
            span = pl.ds(t * LANES, LANES)
            below = [flux_of(t, plane, start + 1) for plane in (6, 3, 1, 0)]
            px[4, rows, span] = wrapped(th[t][2] - th[t][0] + cell[t] - cell_left[t])
            px[5, rows, span] = wrapped(th[t][4] + th[t][6] - below[0] - below[1] + below[2] - below[3])
            px[6, rows, span] = wrapped(th[t][5] + th[t][6] - far[t] + cell[t] - cell_right[t])
            rest = th[t][7]
            for part in range(3):
                head = rest.astype(jnp.bfloat16).astype(jnp.float32)
                px[7 + part, rows, span] = head
                rest = rest - head

    planes = px[...].reshape(10 * EXT, TILES * LANES).astype(jnp.bfloat16)
    lane_place = lax.rem(lane, SIDE) * DEEP
    sub_i = gx * ROWS - HALO + sub

    def cell_inside(y, block):
        j = gy * COLS - HALO + lane_place + y
        i = sub_i + 8 * block
        return (j >= 0) & (j < ny) & (i >= 0) & (i < nx)

    def make_tables(pair, carry):
        two = jnp.dot(
            planes,
            spread_m[:, pl.ds(pl.multiple_of(pair * (2 * LANES), 2 * LANES), 2 * LANES)],
            preferred_element_type=jnp.float32,
        )
        for one in range(2):
            y = 2 * pair + one
            out = two[:, LANES * one : LANES * one + LANES]
            place = lane_place + y
            j = gy * COLS - HALO + place
            for block in range(BLOCKS):
                rows = pl.ds(ROW0 + 8 * block, 8)
                part = [out[which * EXT + 8 * block : which * EXT + 8 * block + 8, :] for which in range(10)]
                for orb in range(4):
                    phf[orb, y, pl.ds(8 * block, 8), :] = part[orb] * (1.0 / QUANTA)
                here = cell_inside(y, block)
                for which, good in (
                    (T2C, here & (j >= 1) & (place >= 1)),
                    (T4C, here & (sub_i + 8 * block + 1 < nx)),
                    (T5C, here & (j + 1 < ny) & (place < SIDE * DEEP - 1)),
                ):
                    c, s = small_turn(part[4 + which // 2], QUANTA)
                    ft[which, y + 1, rows, :] = jnp.where(good, c, 0.0)
                    ft[which + 1, y + 1, rows, :] = jnp.where(good, s, 0.0)
                ft[CPL, y + 1, rows, :] = jnp.where(here, part[7] + part[8] + part[9], 0.0)
        return carry

    lax.fori_loop(0, (DEEP + 1) // 2, make_tables, 0)
    for block in range(BLOCKS):
        rows = pl.ds(ROW0 + 8 * block, 8)
        for which in (T2C, T2S):
            ft[which, DEEP + 1, rows, :] = pltpu.roll(ft[which, 1, rows, :], LANES - 1, 1)
        for which in (T5C, T5S):
            ft[which, 0, rows, :] = pltpu.roll(ft[which, DEEP, rows, :], 1, 1)

    def start_values(blocks):
        def start_one(pair, carry):
            for y in (2 * pair, 2 * pair + 1):
                place = lane_place + y
                beyond = (place < HALO) | (place >= COLS + HALO)
                move = jnp.where(y <= HALO, LANES - HALO - y, SIDE + HALO - y)
                for block in blocks:
                    here = cell_inside(y, block)
                    rows = pl.ds(8 * block, 8)
                    for orb in range(4):
                        angle = jnp.where(beyond, pltpu.roll(halo[block, orb], move, 1), af[orb, y, rows, :])
                        c, s = turn(
                            angle * (0.5 / math.pi) + phf[orb, y, rows, :], 2.0 if orb in (A1, A2) else 1.0
                        )
                        u[0, 2 * orb, y + 1, pl.ds(ROW0 + 8 * block, 8), :] = jnp.where(here, c, 0.0)
                        u[0, 2 * orb + 1, y + 1, pl.ds(ROW0 + 8 * block, 8), :] = jnp.where(here, s, 0.0)
            return carry

        lax.fori_loop(0, (DEEP + 1) // 2, start_one, 0)

    for late, copy in pack_copies:
        if late:
            copy.wait()
    for block in range(BLOCKS):
        for orb in range(4):
            halo[block, orb] = merge(orb, block)
    start_values((1, 2))
    for what, copy in row_copies:
        if what == 2:
            copy.wait()
    spread_angles((0, 3))
    start_values((0, 3))

    def site(buf, orb, y, row):
        rows = pl.ds(ROW0 + row, 8)
        return u[buf, 2 * orb, y + 1, rows, :], u[buf, 2 * orb + 1, y + 1, rows, :]

    def table(which, y, row):
        rows = pl.ds(ROW0 + row, 8)
        return ft[which, y + 1, rows, :], ft[which + 1, y + 1, rows, :]

    def join(buf, row):
        rows = pl.ds(ROW0 + row, 8)
        for part in range(2):
            for orb in (B1, A2):
                u[buf, 2 * orb + part, 0, rows, :] = pltpu.roll(u[buf, 2 * orb + part, DEEP, rows, :], 1, 1)
            for orb in (A1, B2):
                u[buf, 2 * orb + part, DEEP + 1, rows, :] = pltpu.roll(u[buf, 2 * orb + part, 1, rows, :], LANES - 1, 1)

    for block in range(BLOCKS):
        join(0, 8 * block)

    def velocity(y, carry):
        place = lane_place + y
        own = jnp.where((place >= HALO) & (place < COLS + HALO), 0.5, 0.0)
        for block in range(2):
            row = HALO + 8 * block
            v = [None] * 4
            v[A1] = [own * part for part in site(0, B1, y, row - 1)]
            v[B1] = [-own * part for part in site(0, A1, y, row + 1)]
            v[A2] = [-own * part for part in rot(*table(T4C, y, row), site(0, B2, y, row + 1))]
            v[B2] = [own * part for part in rot_back(*table(T4C, y, row - 1), site(0, A2, y, row - 1))]
            for orb in range(4):
                for part in range(2):
                    vel[y, block, 2 * orb + part] = v[orb][part]
        return carry

    lax.fori_loop(0, DEEP, velocity, 0)

    def step_at(src, dst, y, row, first):
        a1, b2, b1, a2 = (site(src, orb, y, row) for orb in range(4))
        hop = ft[CPL, y + 1, pl.ds(ROW0 + row, 8), :]
        new = [None] * 4
        new[A1] = add(b1, site(src, B1, y, row - 1), rot(*table(T2C, y, row), site(src, B1, y - 1, row)))
        new[B1] = add(
            a1,
            site(src, A1, y, row + 1),
            rot_back(*table(T2C, y + 1, row), site(src, A1, y + 1, row)),
            (hop * a2[0], hop * a2[1]),
        )
        new[A2] = add(
            b2,
            rot(*table(T4C, y, row), site(src, B2, y, row + 1)),
            rot(*table(T5C, y, row), site(src, B2, y + 1, row)),
            (hop * b1[0], hop * b1[1]),
        )
        new[B2] = add(
            a2,
            rot_back(*table(T4C, y, row - 1), site(src, A2, y, row - 1)),
            rot_back(*table(T5C, y - 1, row), site(src, A2, y - 1, row)),
        )
        for orb in range(4):
            size = 1.0 if orb in (A1, A2) else 0.25
            for part in range(2):
                value = new[orb][part]
                rows = pl.ds(ROW0 + row, 8)
                if first:
                    value = (0.5 * size) * value
                else:
                    value = (value if size == 1.0 else size * value) - u[dst, 2 * orb + part, y + 1, rows, :]
                u[dst, 2 * orb + part, y + 1, rows, :] = value

    def step(src, dst, rows, first=False):
        def step_two(pair, carry):
            for row in rows:
                step_at(src, dst, 2 * pair, row, first)
                step_at(src, dst, 2 * pair + 1, row, first)
            return carry

        for row in rows:
            step_at(src, dst, DEEP - 1, row, first)
        lax.fori_loop(0, DEEP // 2, step_two, 0)
        for row in rows:
            join(dst, row)

        @pl.when(gx == 0)
        def _():
            for orb in (B1, A2):
                for part in range(2):
                    u[dst, 2 * orb + part, :, pl.ds(ROW0 + HALO - 1, 1), :] = jnp.zeros((DEEP + 2, 1, LANES), jnp.float32)

        @pl.when(gx == gx_size - 1)
        def _():
            for orb in (A1, B2):
                for part in range(2):
                    u[dst, 2 * orb + part, :, pl.ds(ROW0 + HALO + ROWS, 1), :] = jnp.zeros((DEEP + 2, 1, LANES), jnp.float32)

    def gather(k):
        def gather_at(y, sums):
            sums = list(sums)
            for block in range(2):
                for orb in range(4):
                    vr, vi = vel[y, block, 2 * orb], vel[y, block, 2 * orb + 1]
                    for which in range(2):
                        ur, ui = site(which, orb, y, HALO + 8 * block)
                        hist[k + which, y, block, 2 * orb], hist[k + which, y, block, 2 * orb + 1] = ur, ui
                        sums[2 * which] += vr * ur + vi * ui
                        sums[2 * which + 1] += vr * ui - vi * ur
            return tuple(sums)

        def gather_two(pair, sums):
            return gather_at(2 * pair + 1, gather_at(2 * pair, sums))

        sums = gather_at(DEEP - 1, lax.fori_loop(0, DEEP // 2, gather_two, (zero,) * 4))
        for which in range(4):
            mom[2 * k + which] = sums[which]

    far_rows, mid_rows, own_rows = (0, 8, 16, 24), (4, 12, 20), (8, 16)
    step(0, 1, far_rows, first=True)
    gather(0)

    def early(m, carry):
        step(1, 0, far_rows)
        step(0, 1, far_rows)
        gather(2 * m)
        return carry

    def late(m, carry):
        step(1, 0, mid_rows)
        step(0, 1, mid_rows)
        gather(2 * m)
        return carry

    lax.fori_loop(1, 4, early, 0)
    lax.fori_loop(4, TERMS // 2 - 1, late, 0)
    step(1, 0, mid_rows)
    step(0, 1, own_rows)
    gather(TERMS - 2)

    sums = []
    for part in (1, 0):
        for k in range(TERMS):
            sums.append(jnp.sum(mom[2 * k + part], axis=0, keepdims=True))
    state = lax.broadcasted_iota(jnp.int32, (STATES, LANES), 0)
    ones = jnp.where(lane_group == state, 1.0, 0.0)
    local = lax.dot_general(
        ones,
        jnp.concatenate(sums + [jnp.zeros((LANES - 2 * TERMS, LANES), jnp.float32)], axis=0),
        (((1,), (1,)), ((), ())),
        precision=lax.Precision.HIGHEST,
        preferred_element_type=jnp.float32,
    )
    local = jnp.where(lane < TERMS, local, -local) * (1.0 / math.sqrt(4.0 * nx * ny))
    wide = 2 * TERMS
    spread_out = zero
    for q in range(4):
        value = pltpu.roll(local, wide * q, 1) if q else local
        spread_out = jnp.where((lax.rem(sub, 4) == q) & (lane // wide == q), value, spread_out)
    folded = jnp.concatenate(
        [jnp.sum(spread_out[:4], axis=0, keepdims=True), jnp.sum(spread_out[4:], axis=0, keepdims=True)], axis=0
    )

    def spread(value, msg, slots, me, size, peer, send_sem, recv_sem):
        msg[...] = value
        slots[me] = value

        def copy_to(other, slot, d):
            return pltpu.make_async_remote_copy(
                src_ref=msg,
                dst_ref=slots.at[slot],
                send_sem=send_sem.at[d],
                recv_sem=recv_sem.at[slot],
                device_id=peer(other),
                device_id_type=MESH,
            )

        def send(d, carry):
            copy_to(lax.rem(me + d, size), me, d).start()
            return carry

        def finish(d, carry):
            other = lax.rem(me + d, size)
            copy_to(other, me, d).wait_send()
            copy_to(other, other, d).wait_recv()
            return carry

        lax.fori_loop(1, size, send, 0)
        return lambda: lax.fori_loop(1, size, finish, 0)

    def total(slots, size):
        value = slots[0]
        for at in range(1, size):
            value = value + slots[at]
        return value

    def out_copy(orb):
        return pltpu.make_async_copy(outv.at[:, :, orb], evo_h.at[:, :, orb], out_sem.at[orb])

    def evolve(orb, carry):
        def evolve_at(y):
            for block in range(2):
                re, im = zero, zero
                for m in range(TERMS // 2):
                    a, b = ((hist[2 * m + n, y, block, 2 * orb], hist[2 * m + n, y, block, 2 * orb + 1]) for n in range(2))
                    re = re + (EVEN[m] * a[0] - ODD[m] * b[1])
                    im = im + (EVEN[m] * a[1] + ODD[m] * b[0])
                tf[block, y], tf[2 + block, y] = re, im

        def evolve_two(pair, carry):
            evolve_at(2 * pair)
            evolve_at(2 * pair + 1)
            return carry

        evolve_at(DEEP - 1)
        lax.fori_loop(0, DEEP // 2, evolve_two, 0)

        def back(which, carry):
            tiles = [exchanged([tf[which, 8 * t + i] for i in range(8)]) for t in range(2)]
            last = tf[which, DEEP - 1]
            tiles.append([pltpu.roll(last, LANES - SIDE * r, 1) if r else last for r in range(8)])
            for t in range(TILES):
                for r in range(8):
                    tl[which, pl.ds(8 * r, 8), pl.ds(LANES * t, LANES)] = tiles[t][r]
            return carry

        lax.fori_loop(0, 4, back, 0)
        out = moved(tl[...].reshape(4 * 64, TILES * LANES), back_m[...])
        for block in range(2):
            rows = pl.ds(8 * block, 8)
            c = jnp.concatenate([gauge[orb, 0, t, rows, :] for t in range(2)], axis=1)
            s = jnp.concatenate([gauge[orb, 1, t, rows, :] for t in range(2)], axis=1)
            for r in range(8):
                at = 64 * block + 8 * r
                v = rot_back(c, s, (out[at : at + 8, :], out[128 + at : 128 + at + 8, :]))
                outv[0, r, orb, rows, :], outv[1, r, orb, rows, :] = v
        out_copy(orb).start()
        return carry

    finish_1 = spread(folded, msg_1, in_1, place_1, group_1, peer_1, s1_sem, r1_sem)
    lax.fori_loop(0, 2, evolve, 0)
    finish_1()
    finish_2 = spread(total(in_1, group_1), msg_2, in_2, place_2, group_2, peer_2, s2_sem, r2_sem)
    lax.fori_loop(2, 4, evolve, 0)
    finish_2()
    folded = total(in_2, group_2)
    rows = jnp.where(sub < 4, folded[0:1, :], folded[1:2, :])
    result = rows
    for q in range(1, 4):
        result = jnp.where(lax.rem(sub, 4) == q, pltpu.roll(rows, LANES - wide * q, 1), result)
    mom_ref[0] = result[:, :TERMS]
    mom_ref[1] = pltpu.roll(result, LANES - TERMS, 1)[:, :TERMS]
    for orb in range(4):
        out_copy(orb).wait()


def per_device(nx, ny, gx_size, gy_size, angles, bond_flux, coupling):
    f32 = jnp.float32
    tile = (STATES, LANES)
    group_1, group_2 = gx_size // 2, 2 * gy_size
    evolved, moments = pl.pallas_call(
        functools.partial(kernel, nx, ny, gx_size, gy_size),
        out_shape=(
            jax.ShapeDtypeStruct((2, STATES, 4, ROWS, COLS), f32),
            jax.ShapeDtypeStruct((2, STATES, TERMS), f32),
        ),
        in_specs=[pl.BlockSpec(memory_space=pl.ANY)] * 3,
        out_specs=(pl.BlockSpec(memory_space=pl.ANY), pl.BlockSpec(memory_space=pltpu.VMEM)),
        scratch_shapes=[
            pltpu.VMEM((2, STATES, 4, EXT, LANES), f32),
            pltpu.VMEM((2, 7, EXT, LANES), jnp.int32),
            pltpu.VMEM((TILES, 8 * PAD, LANES), f32),
            pltpu.VMEM((2, 8, DEEP + 2, EXT + 2 * ROW0, LANES), f32),
            pltpu.VMEM((TERMS, DEEP, 2, 8) + tile, f32),
            pltpu.VMEM((7, DEEP + 2, EXT + 2 * ROW0, LANES), f32),
            pltpu.VMEM((4, DEEP + 1, EXT, LANES), f32),
            pltpu.VMEM((4, DEEP + 1, EXT, LANES), f32),
            pltpu.VMEM((10, EXT, TILES * LANES), f32),
            pltpu.VMEM((TILES * LANES, (DEEP + 1) * LANES), jnp.bfloat16),
            pltpu.VMEM((COLS, TILES * LANES), jnp.bfloat16),
            pltpu.VMEM((TILES * LANES, COLS), jnp.bfloat16),
            pltpu.VMEM((4, 2, 2, ROWS, LANES), f32),
            pltpu.VMEM((TILES, EXT, LANES), f32),
            pltpu.VMEM((DEEP, 2, 8) + tile, f32),
            pltpu.VMEM((4, DEEP) + tile, f32),
            pltpu.VMEM((4, 64, TILES * LANES), f32),
            pltpu.VMEM((2, STATES, 4, ROWS, COLS), f32),
            pltpu.VMEM((2 * TERMS,) + tile, f32),
            pltpu.VMEM((2, 2, 5) + tile, f32),
            pltpu.VMEM((2, 5) + tile, f32),
            pltpu.VMEM((2, 2, 3) + tile, f32),
            pltpu.VMEM((2, 5) + tile, f32),
            pltpu.VMEM((2, 2, 3) + tile, f32),
            pltpu.VMEM((BLOCKS, 4) + tile, f32),
            pltpu.VMEM((2, LANES), f32),
            pltpu.VMEM((2, LANES), f32),
            pltpu.VMEM((group_1, 2, LANES), f32),
            pltpu.VMEM((group_2, 2, LANES), f32),
            pltpu.SemaphoreType.DMA((2, 3)),
            pltpu.SemaphoreType.DMA((4,)),
            pltpu.SemaphoreType.DMA((2, 2, 3)),
            pltpu.SemaphoreType.DMA((2, 2, 3)),
            pltpu.SemaphoreType.DMA((2, 3, 2)),
            pltpu.SemaphoreType.DMA((2, 3, 2)),
            pltpu.SemaphoreType.DMA((group_1,)),
            pltpu.SemaphoreType.DMA((group_1,)),
            pltpu.SemaphoreType.DMA((group_2,)),
            pltpu.SemaphoreType.DMA((group_2,)),
        ],
        compiler_params=pltpu.CompilerParams(
            collective_id=0, has_side_effects=True, vmem_limit_bytes=60 * 2**20
        ),
        name="evolve",
    )(angles, bond_flux, coupling)
    return evolved, jnp.transpose(moments, (2, 0, 1))


def solution(mesh):
    in_specs = (P(None, None, "gx", "gy"), P(None, "gx", "gy"), P("gx", "gy"))
    out_specs = (P(None, None, None, "gx", "gy"), P())
    gx_size, gy_size = mesh.shape["gx"], mesh.shape["gy"]
    return jax.shard_map(
        functools.partial(per_device, gx_size * ROWS, gy_size * COLS, gx_size, gy_size),
        mesh=mesh,
        in_specs=in_specs,
        out_specs=out_specs,
        check_vma=False,
    )
```

```python
import functools
import math

import jax
import jax.numpy as jnp
import numpy as np
from jax import lax
from jax.experimental import pallas as pl
from jax.experimental.pallas import tpu as pltpu
from jax.sharding import PartitionSpec as P

TERMS = 16
QUANTA = 64
PHASE_SPAN = 12.0

STATES = 8
ROWS = 16
COLS = 256
LANES = 128
HALO = 8
EXT = ROWS + 2 * HALO
PAD = EXT + 8
BLOCKS = EXT // 8
SIDE = 2 * HALO
TILES = 3
DEEP = (COLS + SIDE) // 16
ROW0 = 8
UNROLL = 1
A1, B2, B1, A2 = 0, 1, 2, 3
MESH = pl.DeviceIdType.MESH

T2C, T2S, T4C, T4S, T5C, T5S, CPL = range(7)


def bessel_value(degree, argument):
    running = 0.0
    for number in range(60):
        running += (
            (-1.0) ** number
            * (argument / 2.0) ** (2 * number + degree)
            / (math.factorial(number) * math.factorial(number + degree))
        )
    return running


EVEN = [(1.0 if m == 0 else 2.0) * (-1.0) ** m * bessel_value(2 * m, PHASE_SPAN) for m in range(TERMS // 2)]
ODD = [-2.0 * (-1.0) ** m * bessel_value(2 * m + 1, PHASE_SPAN) for m in range(TERMS // 2)]

def fitted(function, terms):
    nodes = 0.125 - 0.125 * np.cos(math.pi * (np.arange(40) + 0.5) / 40)
    fit = np.polynomial.chebyshev.Chebyshev.fit(nodes, function(np.sqrt(nodes)), terms - 1, domain=[0.0, 0.25])
    return [float(value) for value in fit.convert(kind=np.polynomial.Polynomial).coef]


SIN_COEF = fitted(lambda r: np.sin(math.pi * r) / r, 5)
COS_COEF = fitted(lambda r: np.cos(math.pi * r), 6)


def small_turn(p, unit=1, size=1.0):
    q = p * p
    s, c = SIN_COEF[-1] / unit ** (2 * len(SIN_COEF) - 1), COS_COEF[-1] / unit ** (2 * len(COS_COEF) - 2)
    for power in reversed(range(len(SIN_COEF) - 1)):
        s = s * q + SIN_COEF[power] / unit ** (2 * power + 1)
    for power in reversed(range(len(COS_COEF) - 1)):
        c = c * q + COS_COEF[power] / unit ** (2 * power)
    s = s * p
    twice = (2.0 * size) * s
    return size - twice * s, twice * c


def turn(f, size=1.0):
    return small_turn(f - jnp.floor(f + 0.5), 1, size)


def rot(c, s, v):
    return c * v[0] - s * v[1], s * v[0] + c * v[1]


def rot_back(c, s, v):
    return c * v[0] + s * v[1], c * v[1] - s * v[0]


def add(*pairs):
    re, im = pairs[0]
    for pair in pairs[1:]:
        re, im = re + pair[0], im + pair[1]
    return re, im


def kernel(
    nx, ny, gx_size, gy_size,
    ang_h, flux_h, coup_h, evo_h, mom_ref,
    ang, fli, flf, u, hist, ft, phf, af, px, spread_m, perm_m, back_m, gauge, chi, vel, tf, tl, outv, mom, pack, msg_own, msg_far, got_own, got_far, halo, msg_1, msg_2, in_1, in_2,
    load_sem, out_sem, xs_sem, xr_sem, ps_sem, pr_sem, s1_sem, r1_sem, s2_sem, r2_sem,
):
    gx, gy = lax.axis_index("gx"), lax.axis_index("gy")
    group_1, group_2 = gx_size // 2, 2 * gy_size
    half, place_1 = gx // group_1, lax.rem(gx, group_1)
    place_2 = half * gy_size + gy

    def near(dx, dy):
        return (lax.rem(gx + dx + gx_size, gx_size), lax.rem(gy + dy + gy_size, gy_size))

    def peer_1(other):
        return (half * group_1 + other, gy)

    def peer_2(other):
        return (other // gy_size * group_1 + place_1, lax.rem(other, gy_size))

    lane = lax.broadcasted_iota(jnp.int32, (STATES, LANES), 1)
    sub = lax.broadcasted_iota(jnp.int32, (8, LANES), 0)
    first_lane, last_lane = lane == 0, lane == LANES - 1
    zero = jnp.zeros((STATES, LANES), jnp.float32)

    loads = []
    for t in range(2):
        span = pl.ds(t * LANES, LANES)
        own = pl.ds(HALO, ROWS)
        loads.append(pltpu.make_async_copy(flux_h.at[:, :, span], fli.at[t, :, own, :], load_sem.at[t, 0]))
        loads.append(pltpu.make_async_copy(coup_h.at[:, span], flf.at[t, pl.ds(7 * PAD + HALO, ROWS), :], load_sem.at[t, 1]))
        loads.append(pltpu.make_async_copy(ang_h.at[:, :, :, span], ang.at[t, :, :, own, :], load_sem.at[t, 2]))
    for copy in loads:
        copy.start()

    barrier = pltpu.get_barrier_semaphore()

    def greet(peer, me, size):
        def one(d, carry):
            pl.semaphore_signal(barrier, inc=1, device_id=peer(lax.rem(me + d, size)), device_id_type=MESH)
            return carry

        lax.fori_loop(1, size, one, 0)

    for dx in (-1, 0, 1):
        for dy in (-1, 0, 1):
            if dx or dy:
                pl.semaphore_signal(barrier, inc=1, device_id=near(dx, dy), device_id_type=MESH)
    greet(peer_1, place_1, group_1)
    greet(peer_2, place_2, group_2)

    for t in range(TILES):
        for plane in range(8):
            flf[t, pl.ds(plane * PAD + EXT, 8), :] = zero

    for copy in loads:
        copy.wait()

    def flux_to_float(t, start, count):
        for plane in range(7):
            flf[t, pl.ds(plane * PAD + start, count), :] = fli[t, plane, pl.ds(start, count), :].astype(jnp.float32)

    for t in range(2):
        flux_to_float(t, HALO, ROWS)

    group = lane // HALO

    def packed(side, value_of):
        out = zero
        for r in range(8):
            value = value_of(r)
            move = (SIDE * r + (SIDE if side == 0 else 0)) % LANES
            if move:
                value = pltpu.roll(value, move, 1)
            out = jnp.where(group == 2 * r + 1 - side, value, out)
        return out

    def pack_angles(orb, carry):
        for side in range(2):
            for block in range(2):
                rows = pl.ds(HALO + 8 * block, 8)
                pack[side, block, orb] = packed(side, lambda r: ang[1 - side, r, orb, rows, :])
        return carry

    lax.fori_loop(0, 4, pack_angles, 0)
    for side in range(2):
        for block in range(2):
            pack[side, block, 4] = packed(side, lambda r: flf[1 - side, pl.ds(r * PAD + HALO + 8 * block, 8), :])

    def pushed(value, side):
        return pltpu.roll(value, LANES - HALO if side == 0 else HALO, 1)

    for side in range(2):
        for what in range(5):
            msg_own[side, what] = pack[side, 0, what] + pushed(pack[side, 1, what], side)
        for block in range(2):
            for what in range(2):
                msg_far[side, block, what] = pack[side, block, 2 * what] + pushed(pack[side, block, 2 * what + 1], side)
            msg_far[side, block, 2] = pack[side, block, 4]

    def flux_of(t, plane, start, count=8):
        return flf[t, pl.ds(plane * PAD + start, count), :]

    def wrapped(value):
        return value - QUANTA * jnp.floor(value * (1.0 / QUANTA) + 0.5)

    def cell_phases(t, start, carry):
        if start < HALO:
            run = flux_of(t, 1, start + 1) - flux_of(t, 0, start + 1)
            for reach in (1, 2, 4):
                run = run + jnp.where(sub < 8 - reach, pltpu.roll(run, 8 - reach, 0), 0.0)
        else:
            run = flux_of(t, 0, start) - flux_of(t, 1, start)
            if start == HALO:
                run = jnp.where(sub == 0, 0.0, run)
            for reach in (1, 2, 4):
                run = run + jnp.where(sub >= reach, pltpu.roll(run, reach, 0), 0.0)
            if carry is not None:
                run = run + carry
        run = wrapped(run)
        chi[t, pl.ds(start, 8), :] = run
        th0, th3, th6 = (flux_of(t, plane, start) for plane in (0, 3, 6))
        rows = pl.ds(start, 8)
        span = pl.ds(t * LANES, LANES)
        px[A1, rows, span] = wrapped(run - th0 + QUANTA // 2)
        px[B2, rows, span] = wrapped(th6 + th3 + run + QUANTA // 2)
        px[B1, rows, span] = run
        px[A2, rows, span] = wrapped(th6 + run)
        return jnp.broadcast_to(run[7:8, :], (8, LANES))

    carries = []
    for t in range(2):
        carry = None
        for start in (HALO, HALO + 8):
            carry = cell_phases(t, start, carry)
            for orb in range(4):
                c, s = small_turn(px[orb, pl.ds(start, 8), pl.ds(t * LANES, LANES)], QUANTA)
                if orb in (A1, A2):
                    c, s = 0.5 * c, 0.5 * s
                gauge[orb, 0, t, pl.ds(start - HALO, 8), :] = c
                gauge[orb, 1, t, pl.ds(start - HALO, 8), :] = s
        carries.append(carry)

    def row_place(shape):
        at = lax.broadcasted_iota(jnp.int32, shape, 0)
        return jnp.where(at < COLS + HALO, at + HALO, jnp.where(at < COLS + SIDE, at - COLS - HALO, -1))

    def one_hot(here):
        return jnp.where(here, 1.0, 0.0).astype(jnp.bfloat16)

    at_row = row_place((TILES * LANES, LANES))
    at_lane = lax.rem(lax.broadcasted_iota(jnp.int32, (TILES * LANES, LANES), 1), SIDE) * DEEP

    def make_spread(y, carry):
        spread_m[:, pl.ds(pl.multiple_of(y * LANES, LANES), LANES)] = one_hot(at_row == at_lane + y)
        return carry

    lax.fori_loop(0, DEEP + 1, make_spread, 0)
    wide = lax.broadcasted_iota(jnp.int32, (COLS, TILES * LANES), 1)
    tall = lax.broadcasted_iota(jnp.int32, (COLS, TILES * LANES), 0)
    perm_m[...] = one_hot((tall + HALO == lax.rem(wide, SIDE) * DEEP + wide // SIDE) & (wide < SIDE * DEEP))
    wide = lax.broadcasted_iota(jnp.int32, (TILES * LANES, COLS), 1)
    tall = lax.broadcasted_iota(jnp.int32, (TILES * LANES, COLS), 0)
    back_m[...] = one_hot((wide + HALO == lax.rem(tall, SIDE) * DEEP + tall // SIDE) & (tall < SIDE * DEEP))

    def moved(value, matrix):
        parts = []
        for _ in range(3):
            parts.append(value.astype(jnp.bfloat16))
            value = value - parts[-1].astype(jnp.float32)
        out = jnp.dot(jnp.concatenate(parts, axis=0), matrix, preferred_element_type=jnp.float32)
        size = value.shape[0]
        return out[:size] + out[size : 2 * size] + out[2 * size :]

    lane_group = lane // SIDE

    def exchanged(values):
        values = list(values)
        for s in (1, 2, 4):
            keep = (lane_group // s) % 2 == 0
            for i in range(8):
                if not i & s:
                    one, two = values[i], values[i | s]
                    values[i] = jnp.where(keep, one, pltpu.roll(two, SIDE * s, 1))
                    values[i | s] = jnp.where(keep, pltpu.roll(one, LANES - SIDE * s, 1), two)
        return values

    def spread_angles(blocks):
        def spread_orbs(pair, carry):
            orbs = [2 * pair, 2 * pair + 1]
            places = [(orb, block) for orb in orbs for block in blocks]
            value = jnp.concatenate(
                [
                    jnp.concatenate(
                        [ang[t, :, orb, pl.ds(8 * block, 8), :].reshape(STATES * 8, LANES) for t in range(2)], axis=1
                    )
                    for orb, block in places
                ],
                axis=0,
            )
            out = moved(value, perm_m[...])
            for which, (orb, block) in enumerate(places):
                parts = [
                    [
                        out[64 * which + 8 * r : 64 * which + 8 * r + 8, LANES * t : LANES * t + LANES]
                        for r in range(8)
                    ]
                    for t in range(TILES)
                ]
                deep = exchanged(parts[0]) + exchanged(parts[1])
                last = parts[2][0]
                for r in range(1, 8):
                    last = jnp.where(lane_group == r, pltpu.roll(parts[2][r], SIDE * r, 1), last)
                for y, value in enumerate(deep + [last]):
                    af[orb, y, pl.ds(8 * block, 8), :] = value
            return carry

        lax.fori_loop(0, 2, spread_orbs, 0)

    spread_angles((1, 2))

    pl.semaphore_wait(barrier, 8 + group_1 - 1 + group_2 - 1)

    row_copies = []
    for side, dx in ((0, 1), (1, -1)):
        src_rows = pl.ds(ROWS - HALO, HALO) if side == 0 else pl.ds(0, HALO)
        low = 0 if side == 0 else HALO + ROWS
        for t in range(2):
            span = pl.ds(t * LANES, LANES)
            for what, (src, dst) in enumerate(
                (
                    (flux_h.at[:, src_rows, span], fli.at[t, :, pl.ds(low, HALO), :]),
                    (coup_h.at[src_rows, span], flf.at[t, pl.ds(7 * PAD + low, HALO), :]),
                    (ang_h.at[:, :, src_rows, span], ang.at[t, :, :, pl.ds(low, HALO), :]),
                )
            ):
                row_copies.append(
                    (
                        what,
                        pltpu.make_async_remote_copy(
                            src_ref=src,
                            dst_ref=dst,
                            send_sem=xs_sem.at[side, t, what],
                            recv_sem=xr_sem.at[side, t, what],
                            device_id=near(dx, 0),
                            device_id_type=MESH,
                        ),
                    )
                )
    pack_copies = []
    for side, dy in ((0, 1), (1, -1)):
        for dx, src, dst, cut in (
            (0, msg_own.at[side], got_own.at[side], 4),
            (1, msg_far.at[side, 1], got_far.at[side, 0], 2),
            (-1, msg_far.at[side, 0], got_far.at[side, 1], 2),
        ):
            for late, part in enumerate((pl.ds(cut, 1), pl.ds(0, cut))):
                pack_copies.append(
                    (
                        late,
                        pltpu.make_async_remote_copy(
                            src_ref=src.at[part],
                            dst_ref=dst.at[part],
                            send_sem=ps_sem.at[side, 1 - dx, late],
                            recv_sem=pr_sem.at[side, 1 - dx, late],
                            device_id=near(dx, dy),
                            device_id_type=MESH,
                        ),
                    )
                )
    for late, copy in pack_copies:
        if not late:
            copy.start()
    for what, copy in row_copies:
        if what < 2:
            copy.start()
    for late, copy in pack_copies:
        if late:
            copy.start()
    for what, copy in row_copies:
        if what == 2:
            copy.start()


    for what, copy in row_copies:
        if what < 2:
            copy.wait()
    for t in range(2):
        for start in (0, HALO + ROWS):
            flux_to_float(t, start, HALO)
            cell_phases(t, start, carries[t])
    for late, copy in pack_copies:
        if not late:
            copy.wait()

    beside = lax.rem(lane, SIDE)

    def pulled(value, side):
        return pltpu.roll(value, HALO if side == 0 else LANES - HALO, 1)

    def merge(what, block):
        sides = []
        for side in range(2):
            if block in (1, 2):
                value = got_own[side, what]
                sides.append(pulled(value, side) if block == 2 else value)
            else:
                value = got_far[side, 0 if block == 0 else 1, 2 if what == 4 else what // 2]
                sides.append(pulled(value, side) if what in (1, 3) else value)
        return jnp.where(beside < HALO, sides[1], sides[0])

    for block in range(BLOCKS):
        values = merge(4, block)
        for which in range(8):
            move = (LANES - SIDE * which) % LANES
            flf[2, pl.ds(which * PAD + 8 * block, 8), :] = pltpu.roll(values, move, 1) if move else values
    carry = None
    for start in (HALO, HALO + 8, HALO + ROWS, 0):
        carry = cell_phases(2, start, carry)

    def right(values):
        rolled = [pltpu.roll(value, 1, 1) for value in values]
        edges = [pltpu.roll(values[2], LANES - SIDE + 1, 1), rolled[0], rolled[1]]
        return [jnp.where(first_lane, edges[t], rolled[t]) for t in range(TILES)]

    def left(values):
        rolled = [pltpu.roll(value, LANES - 1, 1) for value in values]
        edge = pltpu.roll(values[0], SIDE - 1, 1)
        return [
            jnp.where(last_lane, rolled[1], rolled[0]),
            jnp.where(last_lane, rolled[2], rolled[1]),
            jnp.where(lane == SIDE - 1, edge, rolled[2]),
        ]

    for start in range(0, EXT, 8):
        rows = pl.ds(start, 8)
        th = [[flux_of(t, plane, start) for plane in range(8)] for t in range(TILES)]
        cell = [chi[t, rows, :] for t in range(TILES)]
        cell_left, cell_right = right(cell), left(cell)
        far = left([th[t][6] + th[t][3] for t in range(TILES)])
        for t in range(TILES):
            span = pl.ds(t * LANES, LANES)
            below = [flux_of(t, plane, start + 1) for plane in (6, 3, 1, 0)]
            px[4, rows, span] = wrapped(th[t][2] - th[t][0] + cell[t] - cell_left[t])
            px[5, rows, span] = wrapped(th[t][4] + th[t][6] - below[0] - below[1] + below[2] - below[3])
            px[6, rows, span] = wrapped(th[t][5] + th[t][6] - far[t] + cell[t] - cell_right[t])
            rest = th[t][7]
            for part in range(3):
                head = rest.astype(jnp.bfloat16).astype(jnp.float32)
                px[7 + part, rows, span] = head
                rest = rest - head

    planes = px[...].reshape(10 * EXT, TILES * LANES).astype(jnp.bfloat16)
    lane_place = lax.rem(lane, SIDE) * DEEP
    sub_i = gx * ROWS - HALO + sub

    def cell_inside(y, block):
        j = gy * COLS - HALO + lane_place + y
        i = sub_i + 8 * block
        return (j >= 0) & (j < ny) & (i >= 0) & (i < nx)

    def make_tables(pair, carry):
        two = jnp.dot(
            planes,
            spread_m[:, pl.ds(pl.multiple_of(pair * (2 * LANES), 2 * LANES), 2 * LANES)],
            preferred_element_type=jnp.float32,
        )
        for one in range(2):
            y = 2 * pair + one
            out = two[:, LANES * one : LANES * one + LANES]
            place = lane_place + y
            j = gy * COLS - HALO + place
            for block in range(BLOCKS):
                rows = pl.ds(ROW0 + 8 * block, 8)
                part = [out[which * EXT + 8 * block : which * EXT + 8 * block + 8, :] for which in range(10)]
                for orb in range(4):
                    phf[orb, y, pl.ds(8 * block, 8), :] = part[orb] * (1.0 / QUANTA)
                here = cell_inside(y, block)
                for which, good in (
                    (T2C, here & (j >= 1) & (place >= 1)),
                    (T4C, here & (sub_i + 8 * block + 1 < nx)),
                    (T5C, here & (j + 1 < ny) & (place < SIDE * DEEP - 1)),
                ):
                    c, s = small_turn(part[4 + which // 2], QUANTA)
                    ft[which, y + 1, rows, :] = jnp.where(good, c, 0.0)
                    ft[which + 1, y + 1, rows, :] = jnp.where(good, s, 0.0)
                ft[CPL, y + 1, rows, :] = jnp.where(here, part[7] + part[8] + part[9], 0.0)
        return carry

    lax.fori_loop(0, (DEEP + 1) // 2, make_tables, 0)
    for block in range(BLOCKS):
        rows = pl.ds(ROW0 + 8 * block, 8)
        for which in (T2C, T2S):
            ft[which, DEEP + 1, rows, :] = pltpu.roll(ft[which, 1, rows, :], LANES - 1, 1)
        for which in (T5C, T5S):
            ft[which, 0, rows, :] = pltpu.roll(ft[which, DEEP, rows, :], 1, 1)

    def start_values(blocks):
        def start_one(pair, carry):
            for y in (2 * pair, 2 * pair + 1):
                place = lane_place + y
                beyond = (place < HALO) | (place >= COLS + HALO)
                move = jnp.where(y <= HALO, LANES - HALO - y, SIDE + HALO - y)
                for block in blocks:
                    here = cell_inside(y, block)
                    rows = pl.ds(8 * block, 8)
                    for orb in range(4):
                        angle = jnp.where(beyond, pltpu.roll(halo[block, orb], move, 1), af[orb, y, rows, :])
                        c, s = turn(
                            angle * (0.5 / math.pi) + phf[orb, y, rows, :], 2.0 if orb in (A1, A2) else 1.0
                        )
                        u[0, 2 * orb, y + 1, pl.ds(ROW0 + 8 * block, 8), :] = jnp.where(here, c, 0.0)
                        u[0, 2 * orb + 1, y + 1, pl.ds(ROW0 + 8 * block, 8), :] = jnp.where(here, s, 0.0)
            return carry

        lax.fori_loop(0, (DEEP + 1) // 2, start_one, 0)

    for late, copy in pack_copies:
        if late:
            copy.wait()
    for block in range(BLOCKS):
        for orb in range(4):
            halo[block, orb] = merge(orb, block)
    start_values((1, 2))
    for what, copy in row_copies:
        if what == 2:
            copy.wait()
    spread_angles((0, 3))
    start_values((0, 3))

    def site(buf, orb, y, row):
        rows = pl.ds(ROW0 + row, 8)
        return u[buf, 2 * orb, y + 1, rows, :], u[buf, 2 * orb + 1, y + 1, rows, :]

    def table(which, y, row):
        rows = pl.ds(ROW0 + row, 8)
        return ft[which, y + 1, rows, :], ft[which + 1, y + 1, rows, :]

    def join(buf, row):
        rows = pl.ds(ROW0 + row, 8)
        for part in range(2):
            for orb in (B1, A2):
                u[buf, 2 * orb + part, 0, rows, :] = pltpu.roll(u[buf, 2 * orb + part, DEEP, rows, :], 1, 1)
            for orb in (A1, B2):
                u[buf, 2 * orb + part, DEEP + 1, rows, :] = pltpu.roll(u[buf, 2 * orb + part, 1, rows, :], LANES - 1, 1)

    for block in range(BLOCKS):
        join(0, 8 * block)

    def velocity(y, carry):
        place = lane_place + y
        own = jnp.where((place >= HALO) & (place < COLS + HALO), 0.5, 0.0)
        for block in range(2):
            row = HALO + 8 * block
            v = [None] * 4
            v[A1] = [own * part for part in site(0, B1, y, row - 1)]
            v[B1] = [-own * part for part in site(0, A1, y, row + 1)]
            v[A2] = [-own * part for part in rot(*table(T4C, y, row), site(0, B2, y, row + 1))]
            v[B2] = [own * part for part in rot_back(*table(T4C, y, row - 1), site(0, A2, y, row - 1))]
            for orb in range(4):
                for part in range(2):
                    vel[y, block, 2 * orb + part] = v[orb][part]
        return carry

    lax.fori_loop(0, DEEP, velocity, 0)

    def step_at(src, dst, y, row, first):
        a1, b2, b1, a2 = (site(src, orb, y, row) for orb in range(4))
        hop = ft[CPL, y + 1, pl.ds(ROW0 + row, 8), :]
        new = [None] * 4
        new[A1] = add(b1, site(src, B1, y, row - 1), rot(*table(T2C, y, row), site(src, B1, y - 1, row)))
        new[B1] = add(
            a1,
            site(src, A1, y, row + 1),
            rot_back(*table(T2C, y + 1, row), site(src, A1, y + 1, row)),
            (hop * a2[0], hop * a2[1]),
        )
        new[A2] = add(
            b2,
            rot(*table(T4C, y, row), site(src, B2, y, row + 1)),
            rot(*table(T5C, y, row), site(src, B2, y + 1, row)),
            (hop * b1[0], hop * b1[1]),
        )
        new[B2] = add(
            a2,
            rot_back(*table(T4C, y, row - 1), site(src, A2, y, row - 1)),
            rot_back(*table(T5C, y - 1, row), site(src, A2, y - 1, row)),
        )
        for orb in range(4):
            size = 1.0 if orb in (A1, A2) else 0.25
            for part in range(2):
                value = new[orb][part]
                rows = pl.ds(ROW0 + row, 8)
                if first:
                    value = (0.5 * size) * value
                else:
                    value = (value if size == 1.0 else size * value) - u[dst, 2 * orb + part, y + 1, rows, :]
                u[dst, 2 * orb + part, y + 1, rows, :] = value

    def step(src, dst, rows, first=False, last=False):
        def step_two(pair, carry):
            for row in rows:
                step_at(src, dst, 2 * pair, row, first)
                step_at(src, dst, 2 * pair + 1, row, first)
            return carry

        for row in rows:
            step_at(src, dst, DEEP - 1, row, first)
        lax.fori_loop(0, DEEP // 2, step_two, 0)
        if last:
            return
        for row in rows:
            join(dst, row)

        @pl.when(gx == 0)
        def _():
            for orb in (B1, A2):
                for part in range(2):
                    u[dst, 2 * orb + part, :, pl.ds(ROW0 + HALO - 1, 1), :] = jnp.zeros((DEEP + 2, 1, LANES), jnp.float32)

        @pl.when(gx == gx_size - 1)
        def _():
            for orb in (A1, B2):
                for part in range(2):
                    u[dst, 2 * orb + part, :, pl.ds(ROW0 + HALO + ROWS, 1), :] = jnp.zeros((DEEP + 2, 1, LANES), jnp.float32)

    def gather(k):
        def gather_at(y, sums):
            sums = list(sums)
            for block in range(2):
                for orb in range(4):
                    vr, vi = vel[y, block, 2 * orb], vel[y, block, 2 * orb + 1]
                    for which in range(2):
                        ur, ui = site(which, orb, y, HALO + 8 * block)
                        hist[k + which, y, block, 2 * orb], hist[k + which, y, block, 2 * orb + 1] = ur, ui
                        sums[2 * which] += vr * ur + vi * ui
                        sums[2 * which + 1] += vr * ui - vi * ur
            return tuple(sums)

        def gather_two(pair, sums):
            return gather_at(2 * pair + 1, gather_at(2 * pair, sums))

        sums = gather_at(DEEP - 1, lax.fori_loop(0, DEEP // 2, gather_two, (zero,) * 4))
        for which in range(4):
            mom[2 * k + which] = sums[which]

    far_rows, mid_rows, own_rows = (0, 8, 16, 24), (4, 12, 20), (8, 16)
    step(0, 1, far_rows, first=True)
    gather(0)

    def early(m, carry):
        step(1, 0, far_rows)
        step(0, 1, far_rows)
        gather(2 * m)
        return carry

    def late(m, carry):
        step(0, 1, mid_rows)
        gather(2 * m)
        step(1, 0, mid_rows)
        return carry

    lax.fori_loop(1, 3, early, 0)
    step(1, 0, far_rows)
    lax.fori_loop(3, TERMS // 2 - 1, late, 0)
    step(0, 1, own_rows, last=True)
    gather(TERMS - 2)

    sums = []
    for part in (1, 0):
        for k in range(TERMS):
            sums.append(jnp.sum(mom[2 * k + part], axis=0, keepdims=True))
    state = lax.broadcasted_iota(jnp.int32, (STATES, LANES), 0)
    ones = jnp.where(lane_group == state, 1.0, 0.0)
    local = lax.dot_general(
        ones,
        jnp.concatenate(sums + [jnp.zeros((LANES - 2 * TERMS, LANES), jnp.float32)], axis=0),
        (((1,), (1,)), ((), ())),
        precision=lax.Precision.HIGHEST,
        preferred_element_type=jnp.float32,
    )
    local = jnp.where(lane < TERMS, local, -local) * (1.0 / math.sqrt(4.0 * nx * ny))
    wide = 2 * TERMS
    spread_out = zero
    for q in range(4):
        value = pltpu.roll(local, wide * q, 1) if q else local
        spread_out = jnp.where((lax.rem(sub, 4) == q) & (lane // wide == q), value, spread_out)
    folded = jnp.concatenate(
        [jnp.sum(spread_out[:4], axis=0, keepdims=True), jnp.sum(spread_out[4:], axis=0, keepdims=True)], axis=0
    )

    def spread(value, msg, slots, me, size, peer, send_sem, recv_sem):
        msg[...] = value
        slots[me] = value

        def copy_to(other, slot, d):
            return pltpu.make_async_remote_copy(
                src_ref=msg,
                dst_ref=slots.at[slot],
                send_sem=send_sem.at[d],
                recv_sem=recv_sem.at[slot],
                device_id=peer(other),
                device_id_type=MESH,
            )

        def send(d, carry):
            copy_to(lax.rem(me + d, size), me, d).start()
            return carry

        def finish(d, carry):
            other = lax.rem(me + d, size)
            copy_to(other, me, d).wait_send()
            copy_to(other, other, d).wait_recv()
            return carry

        lax.fori_loop(1, size, send, 0)
        return lambda: lax.fori_loop(1, size, finish, 0)

    def total(slots, size):
        value = slots[0]
        for at in range(1, size):
            value = value + slots[at]
        return value

    def out_copy(orb):
        return pltpu.make_async_copy(outv.at[:, :, orb], evo_h.at[:, :, orb], out_sem.at[orb])

    def evolve(orb, carry):
        def evolve_at(y):
            for block in range(2):
                re, im = zero, zero
                for m in range(TERMS // 2):
                    a, b = ((hist[2 * m + n, y, block, 2 * orb], hist[2 * m + n, y, block, 2 * orb + 1]) for n in range(2))
                    re = re + (EVEN[m] * a[0] - ODD[m] * b[1])
                    im = im + (EVEN[m] * a[1] + ODD[m] * b[0])
                tf[block, y], tf[2 + block, y] = re, im

        def evolve_two(pair, carry):
            evolve_at(2 * pair)
            evolve_at(2 * pair + 1)
            return carry

        evolve_at(DEEP - 1)
        lax.fori_loop(0, DEEP // 2, evolve_two, 0)

        def back(which, carry):
            tiles = [exchanged([tf[which, 8 * t + i] for i in range(8)]) for t in range(2)]
            last = tf[which, DEEP - 1]
            tiles.append([pltpu.roll(last, LANES - SIDE * r, 1) if r else last for r in range(8)])
            for t in range(TILES):
                for r in range(8):
                    tl[which, pl.ds(8 * r, 8), pl.ds(LANES * t, LANES)] = tiles[t][r]
            return carry

        lax.fori_loop(0, 4, back, 0)
        out = moved(tl[...].reshape(4 * 64, TILES * LANES), back_m[...])
        for block in range(2):
            rows = pl.ds(8 * block, 8)
            c = jnp.concatenate([gauge[orb, 0, t, rows, :] for t in range(2)], axis=1)
            s = jnp.concatenate([gauge[orb, 1, t, rows, :] for t in range(2)], axis=1)
            for r in range(8):
                at = 64 * block + 8 * r
                v = rot_back(c, s, (out[at : at + 8, :], out[128 + at : 128 + at + 8, :]))
                outv[0, r, orb, rows, :], outv[1, r, orb, rows, :] = v
        out_copy(orb).start()
        return carry

    finish_1 = spread(folded, msg_1, in_1, place_1, group_1, peer_1, s1_sem, r1_sem)
    lax.fori_loop(0, 2, evolve, 0)
    finish_1()
    finish_2 = spread(total(in_1, group_1), msg_2, in_2, place_2, group_2, peer_2, s2_sem, r2_sem)
    lax.fori_loop(2, 4, evolve, 0)
    finish_2()
    folded = total(in_2, group_2)
    rows = jnp.where(sub < 4, folded[0:1, :], folded[1:2, :])
    result = rows
    for q in range(1, 4):
        result = jnp.where(lax.rem(sub, 4) == q, pltpu.roll(rows, LANES - wide * q, 1), result)
    mom_ref[0] = result[:, :TERMS]
    mom_ref[1] = pltpu.roll(result, LANES - TERMS, 1)[:, :TERMS]
    for orb in range(4):
        out_copy(orb).wait()


def per_device(nx, ny, gx_size, gy_size, angles, bond_flux, coupling):
    f32 = jnp.float32
    tile = (STATES, LANES)
    group_1, group_2 = gx_size // 2, 2 * gy_size
    evolved, moments = pl.pallas_call(
        functools.partial(kernel, nx, ny, gx_size, gy_size),
        out_shape=(
            jax.ShapeDtypeStruct((2, STATES, 4, ROWS, COLS), f32),
            jax.ShapeDtypeStruct((2, STATES, TERMS), f32),
        ),
        in_specs=[pl.BlockSpec(memory_space=pl.ANY)] * 3,
        out_specs=(pl.BlockSpec(memory_space=pl.ANY), pl.BlockSpec(memory_space=pltpu.VMEM)),
        scratch_shapes=[
            pltpu.VMEM((2, STATES, 4, EXT, LANES), f32),
            pltpu.VMEM((2, 7, EXT, LANES), jnp.int32),
            pltpu.VMEM((TILES, 8 * PAD, LANES), f32),
            pltpu.VMEM((2, 8, DEEP + 2, EXT + 2 * ROW0, LANES), f32),
            pltpu.VMEM((TERMS, DEEP, 2, 8) + tile, f32),
            pltpu.VMEM((7, DEEP + 2, EXT + 2 * ROW0, LANES), f32),
            pltpu.VMEM((4, DEEP + 1, EXT, LANES), f32),
            pltpu.VMEM((4, DEEP + 1, EXT, LANES), f32),
            pltpu.VMEM((10, EXT, TILES * LANES), f32),
            pltpu.VMEM((TILES * LANES, (DEEP + 1) * LANES), jnp.bfloat16),
            pltpu.VMEM((COLS, TILES * LANES), jnp.bfloat16),
            pltpu.VMEM((TILES * LANES, COLS), jnp.bfloat16),
            pltpu.VMEM((4, 2, 2, ROWS, LANES), f32),
            pltpu.VMEM((TILES, EXT, LANES), f32),
            pltpu.VMEM((DEEP, 2, 8) + tile, f32),
            pltpu.VMEM((4, DEEP) + tile, f32),
            pltpu.VMEM((4, 64, TILES * LANES), f32),
            pltpu.VMEM((2, STATES, 4, ROWS, COLS), f32),
            pltpu.VMEM((2 * TERMS,) + tile, f32),
            pltpu.VMEM((2, 2, 5) + tile, f32),
            pltpu.VMEM((2, 5) + tile, f32),
            pltpu.VMEM((2, 2, 3) + tile, f32),
            pltpu.VMEM((2, 5) + tile, f32),
            pltpu.VMEM((2, 2, 3) + tile, f32),
            pltpu.VMEM((BLOCKS, 4) + tile, f32),
            pltpu.VMEM((2, LANES), f32),
            pltpu.VMEM((2, LANES), f32),
            pltpu.VMEM((group_1, 2, LANES), f32),
            pltpu.VMEM((group_2, 2, LANES), f32),
            pltpu.SemaphoreType.DMA((2, 3)),
            pltpu.SemaphoreType.DMA((4,)),
            pltpu.SemaphoreType.DMA((2, 2, 3)),
            pltpu.SemaphoreType.DMA((2, 2, 3)),
            pltpu.SemaphoreType.DMA((2, 3, 2)),
            pltpu.SemaphoreType.DMA((2, 3, 2)),
            pltpu.SemaphoreType.DMA((group_1,)),
            pltpu.SemaphoreType.DMA((group_1,)),
            pltpu.SemaphoreType.DMA((group_2,)),
            pltpu.SemaphoreType.DMA((group_2,)),
        ],
        compiler_params=pltpu.CompilerParams(
            collective_id=0, has_side_effects=True, vmem_limit_bytes=60 * 2**20
        ),
        name="evolve",
    )(angles, bond_flux, coupling)
    return evolved, jnp.transpose(moments, (2, 0, 1))


def solution(mesh):
    in_specs = (P(None, None, "gx", "gy"), P(None, "gx", "gy"), P("gx", "gy"))
    out_specs = (P(None, None, None, "gx", "gy"), P())
    gx_size, gy_size = mesh.shape["gx"], mesh.shape["gy"]
    return jax.shard_map(
        functools.partial(per_device, gx_size * ROWS, gy_size * COLS, gx_size, gy_size),
        mesh=mesh,
        in_specs=in_specs,
        out_specs=out_specs,
        check_vma=False,
    )
```
